128 devices in a mesh: dp: 8 (over x, y_lo), fsdp: 16 (over y_hi, z, core).
Axes of the slice: x: 4, y: 4 (y_hi: 2, y_lo: 2; y = y_hi * 2 + y_lo), z: 4, core: 2. Of those that a mesh axis runs over, the one named last changes fastest.
Arguments:
- tokens: bfloat16 [16384, 2048], P(('dp', 'fsdp')), may hold values from -6 to 6
- cotangent: bfloat16 [16384, 2048], P(('dp', 'fsdp')), may hold values from -6 to 6
- seq_rows: int32 [8, 2], P('dp'), may hold values from 0 to 128, as said below
- qkv_weight: bfloat16 [2048, 4096], P(('dp', 'fsdp')), may hold values from -0.125 to 0.125
- out_weight: bfloat16 [2048, 2048], P(('dp', 'fsdp')), may hold values from -1 to 1
- attn_gain: bfloat16 [2048], P(('dp', 'fsdp')), may hold values from 0.5 to 1.5
- query_gain: bfloat16 [128], P(('dp', 'fsdp')), may hold values from 0.25 to 1.75
- key_gain: bfloat16 [128], P(('dp', 'fsdp')), may hold values from 0.25 to 1.75
- gate_up_weight: bfloat16 [2048, 12288], P(('dp', 'fsdp')), may hold values from -0.125 to 0.125
- down_weight: bfloat16 [2048, 6144], P(('dp', 'fsdp')), may hold values from -0.078125 to 0.078125
- mlp_gain: bfloat16 [2048], P(('dp', 'fsdp')), may hold values from 0.5 to 1.5
Outputs:
- block_out: bfloat16 [16384, 2048], P(('dp', 'fsdp'))
- tokens_grad: float32 [16384, 2048], P(('dp', 'fsdp'))
- qkv_grad: float32 [2048, 4096], P(('dp', 'fsdp'))
- out_grad: float32 [2048, 2048], P(('dp', 'fsdp'))
- attn_gain_grad: float32 [2048], P(('dp', 'fsdp'))
- query_gain_grad: float32 [128], P(('dp', 'fsdp'))
- key_gain_grad: float32 [128], P(('dp', 'fsdp'))
- gate_up_grad: float32 [2048, 12288], P(('dp', 'fsdp'))
- down_grad: float32 [2048, 6144], P(('dp', 'fsdp'))
- mlp_gain_grad: float32 [2048], P(('dp', 'fsdp'))
The draws below stay inside these ranges and needn't reach their ends.
Inputs may be any that keep to these rules, and one draw needn't show every extreme that they name: Row g of seq_rows lists, for each sequence of dp index g in order, how many rows of it each device of that index holds; nonzero entries come first and are 64 or more; a row sums to 64 or more and to 128 at most; in some row the first entry is 128.
All inputs are finite; a program needn't handle non-finite values.
Results may differ from the reference program's by a relative error of at most 0.03.
Values may be sent and summed in bfloat16 or wider, within the bound.
A program may use at most 512 MiB of HBM per device.

```python
import math
import jax
import jax.numpy as jnp
from jax import lax

D = 2048
QUERY_HEADS = 16
KEY_VALUE_HEADS = 8
HEAD_SIZE = 128
FF = 6144
QUERY_FEATURES = 2048
KEY_FEATURES = 1024
QKVW = 4096
MIN_PIECE = 64
TOK_DEV = 128
SEQ_G = 2
GROUPS = 8
TOKENS = 16384
N_DP = 8
N_FSDP = 16


def draw_seq_rows(key, part):
    key = jax.random.fold_in(key, 7)
    keys_list = jax.random.split(key, 4)
    chosen = jax.random.randint(keys_list[0], (), 0, GROUPS)
    slot_ids = jnp.arange(SEQ_G, dtype=jnp.int32)
    group_ids = jnp.arange(GROUPS, dtype=jnp.int32)
    totals = jax.random.randint(keys_list[1], (GROUPS,), TOK_DEV // 2, TOK_DEV + 1)
    totals = jnp.where(group_ids == chosen, TOK_DEV, totals)
    room = jnp.maximum(totals // MIN_PIECE, 1)
    number = jax.random.randint(keys_list[2], (GROUPS,), 1, room + 1)
    number = jnp.where(group_ids == chosen, 1, number)
    active = (slot_ids[None, :] < number[:, None]).astype(jnp.int32)
    shares_w = jax.random.randint(keys_list[3], (GROUPS, SEQ_G), 1, 64) * active
    extra = totals - number * MIN_PIECE
    share = extra[:, None] * shares_w // jnp.sum(shares_w, axis=1, keepdims=True)
    remain = extra - jnp.sum(share, axis=1)
    result = active * MIN_PIECE + share + jnp.where(slot_ids[None, :] == 0, remain[:, None], 0)
    return result.astype(jnp.int32)


def block_scale(rng, dims, cuts, least, largest):
    level = 1.0
    for dim, shards_of in cuts:
        heights = jax.random.uniform(jax.random.fold_in(jax.random.fold_in(rng, 6), dim), (shards_of,), jnp.float32, least / len(cuts), largest / len(cuts))
        level = level * jnp.repeat(jnp.exp(heights), dims[dim] // shards_of).reshape((-1,) + (1,) * (len(dims) - 1 - dim))
    return level


def centred(key, extent, deviation, reach, cuts=(), kind=jnp.bfloat16):
    entries = deviation * jax.random.normal(key, extent, jnp.float32)
    if cuts:
        entries = entries * block_scale(key, extent, cuts, -0.22, 0.18)
    return jnp.clip(entries, -reach, reach).astype(kind)


def setup_inputs(seed: int = 0) -> dict:
    arg_keys = jax.random.split(jax.random.key(seed), 12)
    return {
        "tokens": centred(arg_keys[0], (TOKENS, D), 1.0, 6.0, ((0, 128),)),
        "cotangent": centred(arg_keys[1], (TOKENS, D), 1.0, 6.0, ((0, 128),)),
        "seq_rows": draw_seq_rows(jax.random.fold_in(arg_keys[11], 71), 0),
        "qkv_weight": centred(arg_keys[3], (D, QKVW), D ** -0.5, 0.125, ((0, 128),)),
        "out_weight": centred(arg_keys[4], (D, QUERY_FEATURES), (QUERY_FEATURES // 64) ** -0.5, 1.0, ((0, 128),)),
        "attn_gain": jnp.clip(1.0 + 0.1 * jax.random.normal(arg_keys[5], (D,), jnp.float32), 0.5, 1.5).astype(jnp.bfloat16),
        "query_gain": jnp.clip(1.0 + 0.15 * jax.random.normal(arg_keys[6], (HEAD_SIZE,), jnp.float32), 0.25, 1.75).astype(jnp.bfloat16),
        "key_gain": jnp.clip(1.0 + 0.15 * jax.random.normal(arg_keys[7], (HEAD_SIZE,), jnp.float32), 0.25, 1.75).astype(jnp.bfloat16),
        "gate_up_weight": centred(arg_keys[8], (D, 2 * FF), D ** -0.5, 0.125, ((0, 128),)),
        "down_weight": centred(arg_keys[9], (D, FF), FF ** -0.5, 0.078125, ((0, 128),)),
        "mlp_gain": jnp.clip(1.0 + 0.1 * jax.random.normal(arg_keys[10], (D,), jnp.float32), 0.5, 1.5).astype(jnp.bfloat16),
    }


highest_prec = lax.Precision.HIGHEST
rope_base = 1000000.0

@jax.custom_vjp
def low(v):
    return lax.optimization_barrier(v.astype(jnp.bfloat16)).astype(jnp.float32)

@jax.custom_vjp
def low_back(v):
    return v

def low_keep(v):
    return (low(v), None)

def low_pass(kept, grad):
    return (grad,)

def back_keep(v):
    return (v, None)

def back_low(kept, grad):
    return (low(grad),)
low.defvjp(low_keep, low_pass)
low_back.defvjp(back_keep, back_low)

def rms_scale(values, gain):
    return values * lax.rsqrt(lax.optimization_barrier(jnp.mean(values * values, axis=-1, keepdims=True)) + 1e-06) * gain

def row_layout(seq_counts, device, token_rows):
    seq_ends = jnp.cumsum(seq_counts).astype(jnp.int32)
    starts = (seq_ends - seq_counts).astype(jnp.int32)
    row_place = jnp.arange(token_rows, dtype=jnp.int32)
    inside = ((row_place[:, None] >= starts[None, :]) & (row_place[:, None] < seq_ends[None, :])).astype(jnp.int32)
    slot_ids = jnp.arange(seq_counts.shape[0], dtype=jnp.int32)
    in_sequence = row_place < seq_ends[-1]
    segment = jnp.where(in_sequence, lax.optimization_barrier(jnp.sum(inside * slot_ids[None, :], axis=1)).astype(jnp.int32), -1)
    length = lax.optimization_barrier(jnp.sum(inside * seq_counts[None, :], axis=1)).astype(jnp.int32)
    seq_begin = lax.optimization_barrier(jnp.sum(inside * starts[None, :], axis=1)).astype(jnp.int32)
    position = (device * length[None, :] + row_place[None, :] - seq_begin[None, :]).astype(jnp.int32)
    return (position, segment.astype(jnp.int32))

def rope_tables(position):
    half_dim = HEAD_SIZE // 2
    frequency = jnp.exp(jnp.arange(half_dim, dtype=jnp.float32) * (-2.0 * math.log(rope_base) / HEAD_SIZE))
    angles = position.astype(jnp.float32)[:, None] * frequency[None, :]
    return (jnp.cos(angles)[:, None, :], jnp.sin(angles)[:, None, :])

def rotate(values, cosine, sine_part):
    half_dim = HEAD_SIZE // 2
    first_half = values[..., :half_dim]
    second_half = values[..., half_dim:]
    return jnp.concatenate([first_half * cosine - second_half * sine_part, second_half * cosine + first_half * sine_part], axis=-1)

def prepare(projected_rows, query_scale, key_scale, cosine, sine_part):
    token_rows = projected_rows.shape[0]
    query_rows = projected_rows[:, :QUERY_FEATURES].reshape(token_rows, QUERY_HEADS, HEAD_SIZE)
    unrotated_keys = projected_rows[:, QUERY_FEATURES:QUERY_FEATURES + KEY_FEATURES].reshape(token_rows, KEY_VALUE_HEADS, HEAD_SIZE)
    unrotated_values = projected_rows[:, QUERY_FEATURES + KEY_FEATURES:].reshape(token_rows, KEY_VALUE_HEADS, HEAD_SIZE)
    query_rows = rotate(rms_scale(query_rows, query_scale), cosine, sine_part)
    unrotated_keys = rotate(rms_scale(unrotated_keys, key_scale), cosine, sine_part)
    return (query_rows, unrotated_keys, unrotated_values)

def swiglu(joined):
    return jax.nn.silu(joined[:, :FF]) * joined[:, FF:]

def group_pass(weights, group_in, seq_counts):
    w_qkv, w_out, gain_a, gain_q, gain_k, w_gate_up, w_down, gain_m = weights
    grouped_rows = TOK_DEV * N_FSDP
    score_scale = HEAD_SIZE ** (-0.5)
    repeat_factor = QUERY_HEADS // KEY_VALUE_HEADS
    position, segment = row_layout(seq_counts, jnp.arange(N_FSDP, dtype=jnp.int32)[:, None], TOK_DEV)
    position = position.reshape(grouped_rows)
    segment = jnp.tile(segment, N_FSDP)
    row_index = jnp.arange(grouped_rows, dtype=jnp.int32)
    visible = (segment[:, None] == segment[None, :]) & (segment[:, None] >= 0) & (position[None, :] <= position[:, None]) | (row_index[:, None] == row_index[None, :])
    normed = low(rms_scale(group_in, gain_a))
    projected_rows = low_back(jnp.dot(normed, w_qkv, precision=highest_prec))
    cosine, sine_part = rope_tables(position)
    query_rows, keys_rot, unrotated_values = prepare(projected_rows, gain_q, gain_k, cosine, sine_part)
    query_rows = low(query_rows)
    keys_rot = low(keys_rot)
    unrotated_values = low(unrotated_values)
    keys_rep = jnp.repeat(keys_rot, repeat_factor, axis=1)
    values_rep = jnp.repeat(unrotated_values, repeat_factor, axis=1)
    raw_scores = low_back(jnp.einsum('thd,shd->hts', query_rows, keys_rep, precision=highest_prec))
    scores = jnp.where(visible[None], raw_scores * score_scale, -1e+30)
    totals = jax.nn.logsumexp(scores, axis=-1, keepdims=True)
    weights_p = low(jnp.exp(scores - totals))
    attended = jnp.einsum('hts,shd->thd', weights_p, values_rep, precision=highest_prec)
    attended = low(low_back(attended)).reshape(grouped_rows, QUERY_FEATURES)
    branch = low_back(jnp.dot(attended, w_out.T, precision=highest_prec))
    middle = group_in + branch
    normed_m = low(rms_scale(middle, gain_m))
    joined = low_back(jnp.dot(normed_m, w_gate_up, precision=highest_prec))
    hidden = low(swiglu(joined))
    mlp_out = low_back(jnp.dot(hidden, w_down.T, precision=highest_prec))
    return middle + mlp_out

def reference(tokens, cotangent, seq_rows, qkv_weight, out_weight, attn_gain, query_gain, key_gain, gate_up_weight, down_weight, mlp_gain):
    inputs_f = tokens.astype(jnp.float32)
    weight_list = (qkv_weight.astype(jnp.float32), out_weight.astype(jnp.float32), attn_gain.astype(jnp.float32), query_gain.astype(jnp.float32), key_gain.astype(jnp.float32), gate_up_weight.astype(jnp.float32), down_weight.astype(jnp.float32), mlp_gain.astype(jnp.float32))
    checked = jax.checkpoint(group_pass)

    def forward(layer_in, w_qkv, w_out, gain_a, gain_q, gain_k, w_gate_up, w_down, gain_m):
        params = (w_qkv, w_out, gain_a, gain_q, gain_k, w_gate_up, w_down, gain_m)
        grouped = layer_in.reshape(N_DP, TOK_DEV * N_FSDP, D)

        def per_group(group_item):
            return checked(params, group_item[0], group_item[1])
        mapped = lax.map(per_group, (grouped, seq_rows))
        return mapped.reshape(N_DP * N_FSDP * TOK_DEV, D)
    result, pull_back = jax.vjp(forward, inputs_f, *weight_list)
    grads = pull_back(cotangent.astype(jnp.float32))
    return (result.astype(jnp.bfloat16), grads[0], grads[1], grads[2], grads[3], grads[4], grads[5], grads[6], grads[7], grads[8])
```

```python
import math

import jax
import jax.numpy as jnp
from jax import lax
from jax.experimental import pallas as pl
from jax.experimental.pallas import tpu as pltpu
from jax.sharding import Mesh
from jax.sharding import PartitionSpec as P

HEAD_SIZE = 128
FF = 6144
ROWS = 128
GROUP = 8
HALF_KEYS = ROWS * GROUP
KEYS = 2 * HALF_KEYS
SCALE = HEAD_SIZE**-0.5
EPS = 1e-6
ROPE_BASE = 1000000.0
AXES = ("x", "yl", "yh", "z", "c")
TP = ("z", "c")
PLANE = ("x", "yl", "yh")
f32 = jnp.float32
bf16 = jnp.bfloat16


def row_layout(seq_counts, device, token_rows):
    seq_ends = jnp.cumsum(seq_counts)
    starts = seq_ends - seq_counts
    row_place = jnp.arange(token_rows, dtype=jnp.int32)
    inside = (
        (row_place[:, None] >= starts[None, :]) & (row_place[:, None] < seq_ends[None, :])
    ).astype(jnp.int32)
    slot_ids = jnp.arange(seq_counts.shape[0], dtype=jnp.int32)
    in_sequence = row_place < seq_ends[-1]
    segment = jnp.where(in_sequence, jnp.sum(inside * slot_ids[None, :], axis=1), -1)
    length = jnp.sum(inside * seq_counts[None, :], axis=1)
    seq_begin = jnp.sum(inside * starts[None, :], axis=1)
    position = device * length[None, :] + row_place[None, :] - seq_begin[None, :]
    return (position, segment)


def rope_tables(position):
    half_dim = HEAD_SIZE // 2
    frequency = jnp.exp(
        jnp.arange(half_dim, dtype=f32) * (-2.0 * math.log(ROPE_BASE) / HEAD_SIZE)
    )
    angles = position.astype(f32)[:, None] * frequency[None, :]
    return (jnp.cos(angles)[:, None, :], jnp.sin(angles)[:, None, :])


def rotate(values, cosine, sine_part):
    half_dim = HEAD_SIZE // 2
    a = values[..., :half_dim]
    b = values[..., half_dim:]
    return jnp.concatenate(
        [a * cosine - b * sine_part, b * cosine + a * sine_part], axis=-1
    )


def rms_scale(values, gain):
    return values * lax.rsqrt(jnp.mean(values * values, axis=-1, keepdims=True) + EPS) * gain


def prepare(projected, q_gain, k_gain, cosine, sine_part):
    rows = projected.shape[0]
    q = projected[:, :256].reshape(rows, 2, HEAD_SIZE)
    k = projected[:, 256:384].reshape(rows, 1, HEAD_SIZE)
    q = rotate(rms_scale(q, q_gain), cosine, sine_part)
    k = rotate(rms_scale(k, k_gain), cosine, sine_part)
    return q, k[:, 0], projected[:, 384:]


def swiglu(joined):
    half = joined.shape[1] // 2
    return jax.nn.silu(joined[:, :half]) * joined[:, half:]


def dot(a, b):
    return jnp.dot(a, b, preferred_element_type=f32)


def dot_nt(a, b):
    return lax.dot_general(a, b, (((1,), (1,)), ((), ())), preferred_element_type=f32)


def dot_tn(a, b):
    return lax.dot_general(a, b, (((0,), (0,)), ((), ())), preferred_element_type=f32)


MESH = pl.DeviceIdType.MESH
HALF = 64
ANY = pl.BlockSpec(memory_space=pl.ANY)
VM = pl.BlockSpec(memory_space=pltpu.VMEM)

def where():
    z = lax.axis_index("z"); c = lax.axis_index("c")
    return z, c, lax.rem(z + 1, 4), lax.rem(z + 3, 4), lax.rem(z + 2, 4)

def greet(z, c, up, dn):
    b = pltpu.get_barrier_semaphore()
    pl.semaphore_signal(b, inc=1, device_id={"z": up}, device_id_type=MESH)
    pl.semaphore_signal(b, inc=1, device_id={"z": dn}, device_id_type=MESH)
    pl.semaphore_signal(b, inc=1, device_id={"c": 1 - c}, device_id_type=MESH)
    pl.semaphore_wait(b, 3)

def ag_kernel(x_ref, o_ref, own_sem, send, recv):
    z, c, up, dn, far = where()
    greet(z, c, up, dn)
    me = 2 * z + c
    own = pltpu.make_async_copy(x_ref, o_ref.at[me], own_sem)
    own.start()
    A, B = pl.ds(0, HALF), pl.ds(HALF, HALF)
    def rc(src, dst, i, to):
        return pltpu.make_async_remote_copy(src, dst, send.at[i], recv.at[i], device_id=to, device_id_type=MESH)
    UP, DN, SIB = {"z": up}, {"z": dn}, {"c": 1 - c}
    s_dn, s_up, s_far = 2 * dn + c, 2 * up + c, 2 * far + c
    cp = [
        rc(x_ref.at[A], o_ref.at[me, A], 0, UP),
        rc(x_ref.at[B], o_ref.at[me, B], 1, UP),
        rc(o_ref.at[s_dn, A], o_ref.at[s_dn, A], 2, UP),
        rc(x_ref.at[B], o_ref.at[me, B], 3, DN),
        rc(x_ref.at[A], o_ref.at[me, A], 4, DN),
        rc(o_ref.at[s_up, B], o_ref.at[s_up, B], 5, DN),
        rc(x_ref, o_ref.at[me], 6, SIB),
        rc(o_ref.at[s_dn], o_ref.at[s_dn], 7, SIB),
        rc(o_ref.at[s_up], o_ref.at[s_up], 8, SIB),
        rc(o_ref.at[s_far, A], o_ref.at[s_far, A], 9, SIB),
        rc(o_ref.at[s_far, B], o_ref.at[s_far, B], 10, SIB),
    ]
    for i in (0, 3, 1, 4, 6):
        cp[i].start()
    cp[0].wait_recv(); cp[2].start()
    cp[3].wait_recv(); cp[5].start()
    cp[1].wait_recv(); cp[7].start()
    cp[4].wait_recv(); cp[8].start()
    cp[2].wait_recv(); cp[9].start()
    cp[5].wait_recv(); cp[10].start()
    for i in (6, 7, 8, 9, 10):
        cp[i].wait_recv()
    for i in range(11):
        cp[i].wait_send()
    own.wait()

def ag(x, cid=0):
    return pl.pallas_call(
        ag_kernel, out_shape=jax.ShapeDtypeStruct((8, ROWS) + x.shape[1:], x.dtype),
        in_specs=[ANY], out_specs=ANY,
        scratch_shapes=[pltpu.SemaphoreType.DMA, pltpu.SemaphoreType.DMA((11,)), pltpu.SemaphoreType.DMA((11,))],
        compiler_params=pltpu.CompilerParams(collective_id=cid, has_side_effects=True, vmem_limit_bytes=32<<20),
    )(x)

def rs_kernel(p_ref, o_ref, sib_in, acc, in_up, in_dn, fwd, send, recv):
    z, c, up, dn, far = where()
    greet(z, c, up, dn)
    A, B = pl.ds(0, HALF), pl.ds(HALF, HALF)
    def rc(src, dst, i, to):
        return pltpu.make_async_remote_copy(src, dst, send.at[i], recv.at[i], device_id=to, device_id_type=MESH)
    UP, DN, SIB = {"z": up}, {"z": dn}, {"c": 1 - c}
    order = (far, up, dn, z)
    sib = [rc(p_ref.at[2 * zz + 1 - c], sib_in.at[k], k, SIB) for k, zz in enumerate(order)]
    for s in sib:
        s.start()
    def add(k):
        sib[k].wait_recv()
        acc[k] = (p_ref[2 * order[k] + c].astype(f32) + sib_in[k].astype(f32)).astype(bf16)
    cp = [
        rc(acc.at[0, A], fwd.at[0], 4, DN),
        rc(acc.at[0, B], fwd.at[1], 5, UP),
        rc(acc.at[1, A], in_dn.at[A], 6, UP),
        rc(acc.at[1, B], in_dn.at[B], 7, UP),
        rc(acc.at[2, B], in_up.at[B], 8, DN),
        rc(acc.at[2, A], in_up.at[A], 9, DN),
    ]
    add(0); cp[0].start(); cp[1].start()
    add(1); cp[2].start()
    add(2); cp[4].start()
    cp[1].wait_recv()
    acc[1, B] = (acc[1, B].astype(f32) + fwd[1].astype(f32)).astype(bf16)
    cp[3].start()
    cp[0].wait_recv()
    acc[2, A] = (acc[2, A].astype(f32) + fwd[0].astype(f32)).astype(bf16)
    cp[5].start()
    sib[3].wait_recv()
    o_ref[...] = p_ref[2 * z + c].astype(f32) + sib_in[3].astype(f32)
    cp[2].wait_recv(); cp[3].wait_recv(); cp[4].wait_recv(); cp[5].wait_recv()
    o_ref[...] += in_up[...].astype(f32) + in_dn[...].astype(f32)
    for s in sib + cp:
        s.wait_send()

def rs(p, cid=1):
    n = p.shape[-1]
    return pl.pallas_call(
        rs_kernel, out_shape=jax.ShapeDtypeStruct((ROWS, n), f32),
        in_specs=[VM], out_specs=VM,
        scratch_shapes=[pltpu.VMEM((4, ROWS, n), bf16), pltpu.VMEM((4, ROWS, n), bf16), pltpu.VMEM((ROWS, n), bf16), pltpu.VMEM((ROWS, n), bf16), pltpu.VMEM((2, HALF, n), bf16),
            pltpu.SemaphoreType.DMA((10,)), pltpu.SemaphoreType.DMA((10,))],
        compiler_params=pltpu.CompilerParams(collective_id=cid, has_side_effects=True, vmem_limit_bytes=48<<20),
    )(p)


def gather_rows(a):
    return ag(a).reshape(HALF_KEYS, a.shape[1])


def scatter_rows(a):
    return rs(a.astype(bf16).reshape(GROUP, ROWS, a.shape[1]))


def gather_weight(a):
    return lax.all_gather(a, PLANE, axis=0, tiled=True)


def scatter_weight(a):
    return lax.psum_scatter(a.astype(bf16), PLANE, scatter_dimension=0, tiled=True)


def swap(a):
    return lax.all_to_all(a, TP, split_axis=0, concat_axis=0, tiled=True)


def norm_back(g, xhat, rstd):
    return rstd * (g - xhat * jnp.mean(g * xhat, axis=-1, keepdims=True))


def chunks(w, parts):
    pieces = []
    at = 0
    for width in parts:
        pieces.append(w[:, at : at + width * GROUP].reshape(16, GROUP, width))
        at += width * GROUP
    return jnp.concatenate(pieces, axis=2)


def unchunk(g, parts):
    pieces = []
    at = 0
    for width in parts:
        pieces.append(g[:, :, at : at + width].transpose(1, 0, 2).reshape(16, GROUP * width))
        at += width
    return jnp.concatenate(pieces, axis=1)


def local(
    tokens,
    cotangent,
    seq_rows,
    qkv_weight,
    out_weight,
    attn_gain,
    query_gain,
    key_gain,
    gate_up_weight,
    down_weight,
    mlp_gain,
):
    yh = lax.axis_index("yh")
    gain_a = attn_gain.astype(f32)[:, None]
    gain_m = mlp_gain.astype(f32)[:, None]
    qkv_f = qkv_weight.astype(f32)
    gate_up_f = gate_up_weight.astype(f32)
    pieces = jnp.concatenate(
        [
            chunks((qkv_f * gain_a).astype(bf16), (256, 128, 128)),
            chunks(out_weight, (256,)),
            chunks((gate_up_f * gain_m).astype(bf16), (768, 768)),
            chunks(down_weight, (768,)),
        ],
        axis=2,
    ).transpose(1, 0, 2)
    mine = swap(pieces).reshape(ROWS, 3072)
    w_qkv = gather_weight(mine[:, :512])
    w_out = gather_weight(mine[:, 512:768])
    w_gate_up = gather_weight(mine[:, 768:2304])
    w_down = gather_weight(mine[:, 2304:])
    gains = lax.all_gather(
        jnp.concatenate([query_gain, key_gain])[None], AXES, axis=0, tiled=True
    ).astype(f32)
    gain_q, gain_k = gains[:, 0], gains[:, 1]

    counts = seq_rows[0]
    position_all, segment = row_layout(counts, jnp.arange(16, dtype=jnp.int32)[:, None], ROWS)
    key_position = position_all.reshape(KEYS)
    own_position = lax.dynamic_slice_in_dim(key_position, yh * HALF_KEYS, HALF_KEYS)
    key_segment = jnp.tile(segment, 16)
    own_segment = jnp.tile(segment, 8)
    query_index = yh * HALF_KEYS + jnp.arange(HALF_KEYS, dtype=jnp.int32)
    key_index = jnp.arange(KEYS, dtype=jnp.int32)
    visible = (own_segment[:, None] == key_segment[None, :]) & (own_segment[:, None] >= 0) & (
        key_position[None, :] <= own_position[:, None]
    ) | (query_index[:, None] == key_index[None, :])
    cosine, sine_part = rope_tables(own_position)

    x = tokens.astype(f32)
    rstd = lax.rsqrt(jnp.mean(x * x, axis=-1, keepdims=True) + EPS)
    xhat = x * rstd
    n_full = gather_rows(xhat.astype(bf16))
    c_full = gather_rows(cotangent)
    projected = dot(n_full, w_qkv)

    def prepare_local(p, gq, gk):
        return prepare(p, gq, gk, cosine, sine_part)

    (q, k, v), prepare_back = jax.vjp(prepare_local, projected, gain_q, gain_k)
    q = q.astype(bf16)
    kv = jnp.concatenate([k.astype(bf16), v.astype(bf16)], axis=1)
    kv_all = lax.all_gather(kv, "yh", axis=0, tiled=True)
    k_all, v_all = kv_all[:, :128], kv_all[:, 128:]
    scores = jnp.einsum("tnd,sd->nts", q, k_all, preferred_element_type=f32)
    scores = jnp.where(visible[None], scores * SCALE, -1e30)
    peak = jnp.max(scores, axis=-1, keepdims=True)
    lse = peak + jnp.log(jnp.sum(jnp.exp(scores - peak), axis=-1, keepdims=True))
    probs = jnp.exp(scores - lse).astype(bf16)
    attended = jnp.einsum("nts,sd->tnd", probs, v_all, preferred_element_type=f32)
    attended = attended.astype(bf16).reshape(HALF_KEYS, 256)
    middle = x + scatter_rows(dot_nt(attended, w_out))

    rstd_m = lax.rsqrt(jnp.mean(middle * middle, axis=-1, keepdims=True) + EPS)
    mhat = middle * rstd_m
    m_full = gather_rows(mhat.astype(bf16))
    joined = dot(m_full, w_gate_up)
    hidden_f, swiglu_back = jax.vjp(swiglu, joined)
    hidden = hidden_f.astype(bf16)
    block_out = (middle + scatter_rows(dot_nt(hidden, w_down))).astype(bf16)
    g_joined = swiglu_back(dot(c_full, w_down))[0].astype(bf16)
    g_mhat = scatter_rows(dot_nt(g_joined, w_gate_up))
    g_middle = cotangent.astype(f32) + norm_back(g_mhat, mhat, rstd_m)
    down_part = scatter_weight(dot_tn(c_full, hidden))
    gate_up_part = scatter_weight(dot_tn(m_full, g_joined))

    b_full = gather_rows(g_middle.astype(bf16))
    g_attended = dot(b_full, w_out).astype(bf16).reshape(HALF_KEYS, 2, HEAD_SIZE)
    out_part = scatter_weight(dot_tn(b_full, attended))
    probs_full = jnp.exp(scores - lse)
    g_probs = jnp.einsum("tnd,sd->nts", g_attended, v_all, preferred_element_type=f32)
    inner = jnp.sum(probs_full * g_probs, axis=-1, keepdims=True)
    g_raw = (probs_full * (g_probs - inner) * SCALE).astype(bf16)
    g_q = jnp.einsum("nts,sd->tnd", g_raw, k_all, preferred_element_type=f32)
    g_k = jnp.einsum("nts,tnd->sd", g_raw, q, preferred_element_type=f32)
    g_v = jnp.einsum(
        "nts,tnd->sd", probs_full.astype(bf16), g_attended, preferred_element_type=f32
    )
    g_kv = lax.psum_scatter(
        jnp.concatenate([g_k, g_v], axis=1).astype(bf16), "yh", scatter_dimension=0, tiled=True
    ).astype(f32)
    g_projected, g_gain_q, g_gain_k = prepare_back((g_q, g_kv[:, :128], g_kv[:, 128:]))
    g_projected = g_projected.astype(bf16)
    g_xhat = scatter_rows(dot_nt(g_projected, w_qkv))
    tokens_grad = g_middle + norm_back(g_xhat, xhat, rstd)
    qkv_part = scatter_weight(dot_tn(n_full, g_projected))

    parts = jnp.concatenate([qkv_part, out_part, gate_up_part, down_part], axis=1)
    owned = swap(parts.reshape(GROUP, 16, 3072)).astype(f32)
    qkv_raw = unchunk(owned[:, :, :512], (256, 128, 128))
    out_grad = unchunk(owned[:, :, 512:768], (256,))
    gate_up_raw = unchunk(owned[:, :, 768:2304], (768, 768))
    down_grad = unchunk(owned[:, :, 2304:], (768,))
    gain_grads = lax.psum_scatter(
        jnp.stack([g_gain_q, g_gain_k], axis=1), AXES, scatter_dimension=0, tiled=True
    )
    return (
        block_out,
        tokens_grad,
        qkv_raw * gain_a,
        out_grad,
        jnp.sum(qkv_raw * qkv_f, axis=1),
        gain_grads[:, 0],
        gain_grads[:, 1],
        gate_up_raw * gain_m,
        down_grad,
        jnp.sum(gate_up_raw * gate_up_f, axis=1),
    )


def solution(mesh):
    fine = Mesh(mesh.devices.reshape(4, 2, 2, 4, 2), AXES)
    rows2 = P(AXES, None)
    rows1 = P(AXES)
    return jax.shard_map(
        local,
        mesh=fine,
        in_specs=(
            rows2,
            rows2,
            P(("x", "yl"), None),
            rows2,
            rows2,
            rows1,
            rows1,
            rows1,
            rows2,
            rows2,
            rows1,
        ),
        out_specs=(
            rows2,
            rows2,
            rows2,
            rows2,
            rows1,
            rows1,
            rows1,
            rows2,
            rows2,
            rows1,
        ),
        check_vma=False,
    )
```

```python
import math

import jax
import jax.numpy as jnp
from jax import lax
from jax.experimental import pallas as pl
from jax.experimental.pallas import tpu as pltpu
from jax.sharding import Mesh
from jax.sharding import PartitionSpec as P

HEAD_SIZE = 128
FF = 6144
ROWS = 128
GROUP = 8
HALF_KEYS = ROWS * GROUP
KEYS = 2 * HALF_KEYS
SCALE = HEAD_SIZE**-0.5
WIDTH = 3200
EPS = 1e-6
ROPE_BASE = 1000000.0
AXES = ("x", "yl", "yh", "z", "c")
TP = ("z", "c")
PLANE = ("x", "yl", "yh")
f32 = jnp.float32
bf16 = jnp.bfloat16


def row_layout(seq_counts, device, token_rows):
    seq_ends = jnp.cumsum(seq_counts)
    starts = seq_ends - seq_counts
    row_place = jnp.arange(token_rows, dtype=jnp.int32)
    inside = (
        (row_place[:, None] >= starts[None, :]) & (row_place[:, None] < seq_ends[None, :])
    ).astype(jnp.int32)
    slot_ids = jnp.arange(seq_counts.shape[0], dtype=jnp.int32)
    in_sequence = row_place < seq_ends[-1]
    segment = jnp.where(in_sequence, jnp.sum(inside * slot_ids[None, :], axis=1), -1)
    length = jnp.sum(inside * seq_counts[None, :], axis=1)
    seq_begin = jnp.sum(inside * starts[None, :], axis=1)
    position = device * length[None, :] + row_place[None, :] - seq_begin[None, :]
    return (position, segment)


def rope_tables(position):
    half_dim = HEAD_SIZE // 2
    frequency = jnp.exp(
        jnp.arange(half_dim, dtype=f32) * (-2.0 * math.log(ROPE_BASE) / HEAD_SIZE)
    )
    angles = position.astype(f32)[:, None] * frequency[None, :]
    return (jnp.cos(angles)[:, None, :], jnp.sin(angles)[:, None, :])


def rotate(values, cosine, sine_part):
    half_dim = HEAD_SIZE // 2
    a = values[..., :half_dim]
    b = values[..., half_dim:]
    return jnp.concatenate(
        [a * cosine - b * sine_part, b * cosine + a * sine_part], axis=-1
    )


def rms_scale(values, gain):
    return values * lax.rsqrt(jnp.mean(values * values, axis=-1, keepdims=True) + EPS) * gain


def prepare(projected, q_gain, k_gain, cosine, sine_part):
    rows = projected.shape[0]
    q = projected[:, :256].reshape(rows, 2, HEAD_SIZE)
    k = projected[:, 256:384].reshape(rows, 1, HEAD_SIZE)
    q = rotate(rms_scale(q, q_gain), cosine, sine_part)
    k = rotate(rms_scale(k, k_gain), cosine, sine_part)
    return q, k[:, 0], projected[:, 384:]


def swiglu(joined):
    half = joined.shape[1] // 2
    return jax.nn.silu(joined[:, :half]) * joined[:, half:]


def dot(a, b):
    return jnp.dot(a, b, preferred_element_type=f32)


def dot_nt(a, b):
    return lax.dot_general(a, b, (((1,), (1,)), ((), ())), preferred_element_type=f32)


def dot_tn(a, b):
    return lax.dot_general(a, b, (((0,), (0,)), ((), ())), preferred_element_type=f32)


MESH = pl.DeviceIdType.MESH
ANY = pl.BlockSpec(memory_space=pl.ANY)
VM = pl.BlockSpec(memory_space=pltpu.VMEM)
SM = pl.BlockSpec(memory_space=pltpu.SMEM)
HALF = 64
LOG2E = 1.4426950408889634


def params(cid=None, mib=56):
    if cid is None:
        return pltpu.CompilerParams(vmem_limit_bytes=mib << 20)
    return pltpu.CompilerParams(
        collective_id=cid, has_side_effects=True, vmem_limit_bytes=mib << 20
    )


def rcopy(src, dst, send, recv, to):
    return pltpu.make_async_remote_copy(
        src, dst, send, recv, device_id=to, device_id_type=MESH
    )


def ring_place():
    z, c = lax.axis_index("z"), lax.axis_index("c")
    return z, c, lax.rem(z + 1, 4), lax.rem(z + 3, 4), lax.rem(z + 2, 4)


def plane_place():
    return lax.axis_index("x"), lax.axis_index("yh") * 2 + lax.axis_index("yl")


def y_slot(y):
    return lax.rem(y, 2) * 2 + y // 2


def to_x(x):
    return {"x": x}


def to_y(y):
    return {"yl": lax.rem(y, 2), "yh": y // 2}


def to_group(j):
    return {"z": j // 2, "c": lax.rem(j, 2)}


def greet(targets):
    barrier = pltpu.get_barrier_semaphore()
    for to in targets:
        pl.semaphore_signal(barrier, inc=1, device_id=to, device_id_type=MESH)
    pl.semaphore_wait(barrier, len(targets))


def ring_targets():
    z, c, up, dn, far = ring_place()
    return [{"z": up}, {"z": dn}, {"c": 1 - c}]


def group_targets(me):
    return [to_group(lax.rem(me + d, GROUP)) for d in range(1, GROUP)]


def plane_targets(x, y):
    return [to_x(lax.rem(x + s, 4)) for s in (1, 2, 3)] + [
        to_y(lax.rem(y + s, 4)) for s in (1, 2, 3)
    ]


class RowGather:
    def __init__(self, src, dst, own_sem, send, recv):
        z, c, up, dn, far = ring_place()
        me = 2 * z + c
        low, high = pl.ds(0, HALF), pl.ds(HALF, HALF)
        s_dn, s_up, s_far = 2 * dn + c, 2 * up + c, 2 * far + c
        to_up, to_dn, to_sib = {"z": up}, {"z": dn}, {"c": 1 - c}
        plan = [
            (src.at[low], dst.at[me, low], to_up),
            (src.at[high], dst.at[me, high], to_up),
            (dst.at[s_dn, low], dst.at[s_dn, low], to_up),
            (src.at[high], dst.at[me, high], to_dn),
            (src.at[low], dst.at[me, low], to_dn),
            (dst.at[s_up, high], dst.at[s_up, high], to_dn),
            (src, dst.at[me], to_sib),
            (dst.at[s_dn], dst.at[s_dn], to_sib),
            (dst.at[s_up], dst.at[s_up], to_sib),
            (dst.at[s_far, low], dst.at[s_far, low], to_sib),
            (dst.at[s_far, high], dst.at[s_far, high], to_sib),
        ]
        self.cp = [rcopy(a, b, send.at[i], recv.at[i], to) for i, (a, b, to) in enumerate(plan)]
        self.own = pltpu.make_async_copy(src, dst.at[me], own_sem)

    def start(self):
        self.own.start()
        for i in (0, 3, 1, 4, 6):
            self.cp[i].start()

    def relay(self):
        cp = self.cp
        cp[0].wait_recv()
        cp[2].start()
        cp[3].wait_recv()
        cp[5].start()
        cp[1].wait_recv()
        cp[7].start()
        cp[4].wait_recv()
        cp[8].start()

    def have_own(self):
        self.own.wait()
        self.cp[6].wait_recv()

    def have_dn(self):
        self.cp[7].wait_recv()

    def have_up(self):
        self.cp[8].wait_recv()

    def have_far(self):
        cp = self.cp
        cp[2].wait_recv()
        cp[9].start()
        cp[5].wait_recv()
        cp[10].start()
        cp[9].wait_recv()
        cp[10].wait_recv()

    def drain(self):
        for c in self.cp:
            c.wait_send()


class Ring:
    def __init__(self, axis, at, block, first, rows, send, recv):
        step = to_x if axis == "x" else to_y
        up, dn = lax.rem(at + 1, 4), lax.rem(at + 3, 4)
        whole = pl.ds(first, rows)
        low, high = pl.ds(first, rows // 2), pl.ds(first + rows // 2, rows // 2)
        plan = [
            (block(at).at[whole], step(up)),
            (block(at).at[whole], step(dn)),
            (block(dn).at[low], step(up)),
            (block(up).at[high], step(dn)),
        ]
        self.cp = [rcopy(r, r, send.at[i], recv.at[i], to) for i, (r, to) in enumerate(plan)]

    def start(self):
        self.cp[0].start()
        self.cp[1].start()

    def relay(self):
        self.cp[0].wait_recv()
        self.cp[2].start()
        self.cp[1].wait_recv()
        self.cp[3].start()

    def finish(self):
        self.cp[2].wait_recv()
        self.cp[3].wait_recv()

    def drain(self):
        for c in self.cp:
            c.wait_send()


class PlaneGather:
    def __init__(self, dst, send, recv):
        x, y = plane_place()
        self.halves = []
        for half in (0, 1):
            first = half * HALF

            def along_x(y_at, x_at):
                return dst.at[x_at, y_slot(y_at)]

            def ring(axis, other, k):
                if axis == "x":
                    block = lambda at: dst.at[at, y_slot(other)]
                    at = x
                else:
                    block = lambda at: dst.at[other, y_slot(at)]
                    at = y
                return Ring(axis, at, block, first, HALF, send.at[half, k], recv.at[half, k])

            axes = ("y", "x") if half == 0 else ("x", "y")
            here, over = (y, x) if half == 0 else (x, y)
            others = [here, lax.rem(here + 3, 4), lax.rem(here + 1, 4), lax.rem(here + 2, 4)]
            self.halves.append(
                [ring(axes[0], over, 0)] + [ring(axes[1], o, 1 + k) for k, o in enumerate(others)]
            )

    def steps(self):
        a, b = self.halves

        def both(k, what):
            getattr(a[k], what)()
            getattr(b[k], what)()

        def one():
            both(0, "start")
            both(1, "start")

        def two():
            both(0, "relay")
            both(2, "start")
            both(3, "start")

        def three():
            both(1, "relay")
            both(0, "finish")
            both(4, "start")

        def four():
            both(2, "relay")
            both(3, "relay")

        def five():
            both(4, "relay")

        return [one, two, three, four, five]

    def finish(self):
        for half in self.halves:
            for k in range(1, 5):
                half[k].finish()
        for half in self.halves:
            for r in half:
                r.drain()


def front_kernel(x_ref, p_ref, n_ref, w_ref, own_sems, g_send, g_recv, s_send, s_recv, w_send, w_recv):
    z, c, up, dn, far = ring_place()
    me = 2 * z + c
    x, y = plane_place()
    greet(group_targets(me) + plane_targets(x, y))
    mine = w_ref.at[x, y_slot(y)]
    rows = pl.ds(pl.multiple_of(16 * me, 16), 16)
    own = pltpu.make_async_copy(p_ref.at[me], mine.at[rows], own_sems.at[0])
    own.start()
    swaps = []
    for d in range(1, GROUP):
        j = lax.rem(me + d, GROUP)
        swaps.append(rcopy(p_ref.at[j], mine.at[rows], s_send.at[d - 1], s_recv.at[d - 1], to_group(j)))
    for s in swaps:
        s.start()
    gather = RowGather(x_ref, n_ref, own_sems.at[1], g_send, g_recv)
    gather.start()
    own.wait()
    for s in swaps:
        s.wait_recv()
    plane = PlaneGather(w_ref, w_send, w_recv)
    steps = plane.steps()
    steps[0]()
    gather.relay()
    steps[1]()
    gather.have_own()
    gather.have_dn()
    gather.have_up()
    gather.have_far()
    for s in steps[2:]:
        s()
    plane.finish()
    gather.drain()
    for s in swaps:
        s.wait_send()


def front(xhat, pieces, cid):
    width = pieces.shape[2]
    dma = pltpu.SemaphoreType.DMA
    return pl.pallas_call(
        front_kernel,
        out_shape=(
            jax.ShapeDtypeStruct((GROUP, ROWS, xhat.shape[1]), bf16),
            jax.ShapeDtypeStruct((4, 4, ROWS, width), bf16),
        ),
        in_specs=[ANY, ANY],
        out_specs=(ANY, ANY),
        scratch_shapes=[
            dma((2,)),
            dma((11,)),
            dma((11,)),
            dma((7,)),
            dma((7,)),
            dma((2, 5, 4)),
            dma((2, 5, 4)),
        ],
        compiler_params=params(cid),
        name="front",
    )(xhat, pieces)


def grads_kernel(p_ref, o_ref, own_a, own_b, in_a, in_b, next_a, next_b, last, own_sems, send1, recv1, send2, recv2, s_send, s_recv):
    z, c, up, dn, far = ring_place()
    me = 2 * z + c
    x, y = plane_place()
    greet(group_targets(me) + plane_targets(x, y))
    low, high = pl.ds(0, HALF), pl.ds(HALF, HALF)
    first_a, first_b = [], []
    for s in (1, 2, 3):
        xt, yt = lax.rem(x + s, 4), lax.rem(y + s, 4)
        first_a.append(rcopy(p_ref.at[xt, :, low], in_a.at[s - 1], send1.at[0, s - 1], recv1.at[0, s - 1], to_x(xt)))
        first_b.append(rcopy(p_ref.at[:, y_slot(yt), high], in_b.at[s - 1], send1.at[1, s - 1], recv1.at[1, s - 1], to_y(yt)))
    for a, b in zip(first_a, first_b):
        a.start()
        b.start()
    get_a = pltpu.make_async_copy(p_ref.at[x, :, low], own_a, own_sems.at[0])
    get_b = pltpu.make_async_copy(p_ref.at[:, y_slot(y), high], own_b, own_sems.at[1])
    get_a.start()
    get_b.start()

    def total(own, arrived, k, r):
        t = own[k, r].astype(f32)
        for s in range(3):
            t += arrived[s, k, r].astype(f32)
        return t

    def sum_first(own, arrived):
        def body(i, carry):
            k, r = i // 4, pl.ds(pl.multiple_of(lax.rem(i, 4) * 16, 16), 16)
            own[k, r] = total(own, arrived, k, r).astype(bf16)
            return carry

        lax.fori_loop(0, 16, body, 0)

    get_a.wait()
    for a in first_a:
        a.wait_recv()
    sum_first(own_a, in_a)
    second_a, second_b = [], []
    for s in (1, 2, 3):
        yt, xt = lax.rem(y + s, 4), lax.rem(x + s, 4)
        second_a.append(rcopy(own_a.at[y_slot(yt)], next_a.at[s - 1], send2.at[0, s - 1], recv2.at[0, s - 1], to_y(yt)))
        second_b.append(rcopy(own_b.at[xt], next_b.at[s - 1], send2.at[1, s - 1], recv2.at[1, s - 1], to_x(xt)))
    for a in second_a:
        a.start()
    get_b.wait()
    for b in first_b:
        b.wait_recv()
    sum_first(own_b, in_b)
    for b in second_b:
        b.start()

    def sum_second(own, k, arrived, first):
        for i in range(4):
            r = pl.ds(16 * i, 16)
            t = own[k, r].astype(f32)
            for s in range(3):
                t += arrived[s, r].astype(f32)
            last[pl.ds(first + 16 * i, 16)] = t.astype(bf16)

    for a in second_a:
        a.wait_recv()
    sum_second(own_a, y_slot(y), next_a, 0)
    for b in second_b:
        b.wait_recv()
    sum_second(own_b, x, next_b, HALF)

    own = pltpu.make_async_copy(last.at[pl.ds(pl.multiple_of(16 * me, 16), 16)], o_ref.at[me], own_sems.at[2])
    own.start()
    swaps = []
    for d in range(1, GROUP):
        j = lax.rem(me + d, GROUP)
        swaps.append(rcopy(last.at[pl.ds(pl.multiple_of(16 * j, 16), 16)], o_ref.at[me], s_send.at[d - 1], s_recv.at[d - 1], to_group(j)))
    for s in swaps:
        s.start()
    own.wait()
    for s in swaps:
        s.wait_recv()
    for s in first_a + first_b + second_a + second_b + swaps:
        s.wait_send()


def scatter_grads(p, cid):
    width = p.shape[1]
    dma = pltpu.SemaphoreType.DMA
    return pl.pallas_call(
        grads_kernel,
        out_shape=jax.ShapeDtypeStruct((GROUP, 16, width), bf16),
        in_specs=[ANY],
        out_specs=ANY,
        scratch_shapes=[
            pltpu.VMEM((4, HALF, width), bf16),
            pltpu.VMEM((4, HALF, width), bf16),
            pltpu.VMEM((3, 4, HALF, width), bf16),
            pltpu.VMEM((3, 4, HALF, width), bf16),
            pltpu.VMEM((3, HALF, width), bf16),
            pltpu.VMEM((3, HALF, width), bf16),
            pltpu.VMEM((ROWS, width), bf16),
            dma((3,)),
            dma((2, 3)),
            dma((2, 3)),
            dma((2, 3)),
            dma((2, 3)),
            dma((7,)),
            dma((7,)),
        ],
        compiler_params=params(cid),
        name="grads",
    )(p.reshape(4, 4, ROWS, width))


def attend_kernel(late_ref, q_ref, kv_ref, okv_ref, qseg_ref, kseg_ref, o_ref, acc, tot):
    for h in range(2):
        cols = pl.ds(128 * h, 128)
        for i in range(4):
            rows = pl.ds(256 * i, 256)
            q = q_ref[rows, cols]
            t = jnp.zeros((256, 1), f32)
            a = jnp.zeros((256, 128), f32)
            for k in range(i + 1):
                keys = pl.ds(256 * k, 256)
                s = dot_nt(q, kv_ref[keys, 0:128])
                ok = qseg_ref[rows, :] == kseg_ref[0:1, keys]
                if k == i:
                    ok &= lax.broadcasted_iota(jnp.int32, (256, 256), 0) >= lax.broadcasted_iota(
                        jnp.int32, (256, 256), 1
                    )
                p = jnp.where(ok, jnp.exp2(s * (SCALE * LOG2E)), 0.0)
                t += jnp.sum(p, axis=1, keepdims=True)
                a += dot(p.astype(bf16), kv_ref[keys, 128:256])
            acc[rows, cols] = a
            tot[h, rows] = t

    @pl.when(late_ref[0] == 1)
    def _():
        for h in range(2):
            cols = pl.ds(128 * h, 128)

            def body(i, carry):
                rows = pl.ds(pl.multiple_of(256 * i, 256), 256)
                q = q_ref[rows, cols]
                t = tot[h, rows]
                a = acc[rows, cols]
                for k in range(4):
                    keys = pl.ds(256 * k, 256)
                    s = dot_nt(q, okv_ref[keys, 0:128])
                    ok = qseg_ref[rows, :] == kseg_ref[1:2, keys]
                    p = jnp.where(ok, jnp.exp2(s * (SCALE * LOG2E)), 0.0)
                    t += jnp.sum(p, axis=1, keepdims=True)
                    a += dot(p.astype(bf16), okv_ref[keys, 128:256])
                tot[h, rows] = t
                acc[rows, cols] = a
                return carry

            lax.fori_loop(0, 4, body, 0)

    for h in range(2):
        cols = pl.ds(128 * h, 128)
        o_ref[:, cols] = (acc[:, cols] / tot[h]).astype(bf16)


def attend(late, q, kv, okv, qseg, kseg):
    return pl.pallas_call(
        attend_kernel,
        out_shape=jax.ShapeDtypeStruct((HALF_KEYS, 256), bf16),
        in_specs=[SM, VM, VM, VM, VM, VM],
        out_specs=VM,
        scratch_shapes=[pltpu.VMEM((HALF_KEYS, 256), f32), pltpu.VMEM((2, HALF_KEYS, 1), f32)],
        compiler_params=params(),
        name="attend",
    )(late, q, kv, okv, qseg, kseg)


def attend_back_kernel(late_ref, q_ref, kv_ref, okv_ref, g_ref, qseg_ref, kseg_ref, gq_ref, gkv_ref, gokv_ref, ps, gps, tot, inn):
    gkv_ref[...] = jnp.zeros_like(gkv_ref)
    gokv_ref[...] = jnp.zeros_like(gokv_ref)

    def weigh(i, h, which, k, diagonal):
        rows, cols = pl.ds(256 * i, 256), pl.ds(128 * h, 128)
        source = okv_ref if which else kv_ref
        keys = pl.ds(pl.multiple_of(256 * k, 256), 256)
        slot = pl.ds(pl.multiple_of(256 * k + 1024 * which, 256), 256)
        s = dot_nt(source[keys, 0:128], q_ref[rows, cols])
        ok = kseg_ref[which, keys] == qseg_ref[0:1, rows]
        if diagonal:
            ok &= lax.broadcasted_iota(jnp.int32, (256, 256), 1) >= lax.broadcasted_iota(
                jnp.int32, (256, 256), 0
            )
        p = jnp.where(ok, jnp.exp2(s * (SCALE * LOG2E)), 0.0)
        gp = dot_nt(source[keys, 128:256], g_ref[rows, cols])
        tot[...] += jnp.sum(p, axis=0, keepdims=True)
        inn[...] += jnp.sum(p * gp, axis=0, keepdims=True)
        ps[slot] = p
        gps[slot] = gp

    def spread(i, h, which, k):
        rows, cols = pl.ds(256 * i, 256), pl.ds(128 * h, 128)
        source, out = (okv_ref, gokv_ref) if which else (kv_ref, gkv_ref)
        keys = pl.ds(pl.multiple_of(256 * k, 256), 256)
        slot = pl.ds(pl.multiple_of(256 * k + 1024 * which, 256), 256)
        p = ps[slot] * tot[...]
        ds = (p * (gps[slot] - inn[...]) * SCALE).astype(bf16)
        out[keys, 0:128] += dot(ds, q_ref[rows, cols])
        out[keys, 128:256] += dot(p.astype(bf16), g_ref[rows, cols])
        gq_ref[rows, cols] += dot_tn(ds, source[keys, 0:128])

    for h in range(2):
        for i in range(4):
            tot[...] = jnp.zeros_like(tot)
            inn[...] = jnp.zeros_like(inn)
            gq_ref[pl.ds(256 * i, 256), pl.ds(128 * h, 128)] = jnp.zeros((256, 128), f32)
            for k in range(i + 1):
                weigh(i, h, 0, k, k == i)

            @pl.when(late_ref[0] == 1)
            def _():
                def body(k, carry):
                    weigh(i, h, 1, k, False)
                    return carry

                lax.fori_loop(0, 4, body, 0)

            inv = 1.0 / tot[...]
            tot[...] = inv
            inn[...] = inn[...] * inv
            for k in range(i + 1):
                spread(i, h, 0, k)

            @pl.when(late_ref[0] == 1)
            def _():
                def body(k, carry):
                    spread(i, h, 1, k)
                    return carry

                lax.fori_loop(0, 4, body, 0)


def attend_back(late, q, kv, okv, g, qseg_row, kseg_col):
    return pl.pallas_call(
        attend_back_kernel,
        out_shape=tuple(jax.ShapeDtypeStruct((HALF_KEYS, 256), f32) for _ in range(3)),
        in_specs=[SM] + [VM] * 6,
        out_specs=(VM, VM, VM),
        scratch_shapes=[
            pltpu.VMEM((KEYS, 256), f32),
            pltpu.VMEM((KEYS, 256), f32),
            pltpu.VMEM((1, 256), f32),
            pltpu.VMEM((1, 256), f32),
        ],
        compiler_params=params(),
        name="attend_back",
    )(late, q, kv, okv, g, qseg_row, kseg_col)


def gather_kernel(x_ref, o_ref, own_sem, send, recv):
    greet(ring_targets())
    g = RowGather(x_ref, o_ref, own_sem, send, recv)
    g.start()
    g.relay()
    g.have_own()
    g.have_dn()
    g.have_up()
    g.have_far()
    g.drain()


def gather_rows(x, cid):
    dma = pltpu.SemaphoreType.DMA
    return pl.pallas_call(
        gather_kernel,
        out_shape=jax.ShapeDtypeStruct((GROUP, ROWS, x.shape[1]), x.dtype),
        in_specs=[ANY],
        out_specs=ANY,
        scratch_shapes=[dma, dma((11,)), dma((11,))],
        compiler_params=params(cid),
        name="gather_rows",
    )(x).reshape(HALF_KEYS, x.shape[1])


def rs_kernel(p_ref, o_ref, sib_in, acc, in_up, in_dn, fwd, send, recv):
    z, c, up, dn, far = ring_place()
    greet(ring_targets())
    A, B = pl.ds(0, HALF), pl.ds(HALF, HALF)
    def rc(src, dst, i, to):
        return pltpu.make_async_remote_copy(src, dst, send.at[i], recv.at[i], device_id=to, device_id_type=MESH)
    UP, DN, SIB = {"z": up}, {"z": dn}, {"c": 1 - c}
    order = (far, up, dn, z)
    sib = [rc(p_ref.at[2 * zz + 1 - c], sib_in.at[k], k, SIB) for k, zz in enumerate(order)]
    for s in sib:
        s.start()
    def add(k):
        sib[k].wait_recv()
        acc[k] = (p_ref[2 * order[k] + c].astype(f32) + sib_in[k].astype(f32)).astype(bf16)
    cp = [
        rc(acc.at[0, A], fwd.at[0], 4, DN),
        rc(acc.at[0, B], fwd.at[1], 5, UP),
        rc(acc.at[1, A], in_dn.at[A], 6, UP),
        rc(acc.at[1, B], in_dn.at[B], 7, UP),
        rc(acc.at[2, B], in_up.at[B], 8, DN),
        rc(acc.at[2, A], in_up.at[A], 9, DN),
    ]
    add(0); cp[0].start(); cp[1].start()
    add(1); cp[2].start()
    add(2); cp[4].start()
    cp[1].wait_recv()
    acc[1, B] = (acc[1, B].astype(f32) + fwd[1].astype(f32)).astype(bf16)
    cp[3].start()
    cp[0].wait_recv()
    acc[2, A] = (acc[2, A].astype(f32) + fwd[0].astype(f32)).astype(bf16)
    cp[5].start()
    sib[3].wait_recv()
    o_ref[...] = p_ref[2 * z + c].astype(f32) + sib_in[3].astype(f32)
    cp[2].wait_recv(); cp[3].wait_recv(); cp[4].wait_recv(); cp[5].wait_recv()
    o_ref[...] += in_up[...].astype(f32) + in_dn[...].astype(f32)
    for s in sib + cp:
        s.wait_send()

def scatter_rows(p, cid):
    n = p.shape[-1]
    p = p.astype(bf16).reshape(GROUP, ROWS, n)
    return pl.pallas_call(
        rs_kernel, out_shape=jax.ShapeDtypeStruct((ROWS, n), f32),
        in_specs=[VM], out_specs=VM,
        scratch_shapes=[pltpu.VMEM((4, ROWS, n), bf16), pltpu.VMEM((4, ROWS, n), bf16), pltpu.VMEM((ROWS, n), bf16), pltpu.VMEM((ROWS, n), bf16), pltpu.VMEM((2, HALF, n), bf16),
            pltpu.SemaphoreType.DMA((10,)), pltpu.SemaphoreType.DMA((10,))],
        compiler_params=pltpu.CompilerParams(collective_id=cid, has_side_effects=True, vmem_limit_bytes=48<<20),
    )(p)


def norm_back(g, xhat, rstd):
    return rstd * (g - xhat * jnp.mean(g * xhat, axis=-1, keepdims=True))


def chunks(w, parts):
    pieces = []
    at = 0
    for width in parts:
        pieces.append(w[:, at : at + width * GROUP].reshape(16, GROUP, width))
        at += width * GROUP
    return jnp.concatenate(pieces, axis=2)


def unchunk(g, parts):
    pieces = []
    at = 0
    for width in parts:
        pieces.append(g[:, :, at : at + width].transpose(1, 0, 2).reshape(16, GROUP * width))
        at += width
    return jnp.concatenate(pieces, axis=1)


def local(
    tokens,
    cotangent,
    seq_rows,
    qkv_weight,
    out_weight,
    attn_gain,
    query_gain,
    key_gain,
    gate_up_weight,
    down_weight,
    mlp_gain,
):
    yh = lax.axis_index("yh")
    gain_a = attn_gain.astype(f32)[:, None]
    gain_m = mlp_gain.astype(f32)[:, None]
    qkv_f = qkv_weight.astype(f32)
    gate_up_f = gate_up_weight.astype(f32)
    head_gains = jnp.broadcast_to(
        jnp.pad(jnp.concatenate([query_gain, key_gain]), (0, 126)), (16, GROUP, 128)
    )
    pieces = jnp.concatenate(
        [
            chunks((qkv_f * gain_a).astype(bf16), (256, 128, 128)),
            head_gains,
            chunks(out_weight, (256,)),
            chunks((gate_up_f * gain_m).astype(bf16), (768, 768)),
            chunks(down_weight, (768,)),
        ],
        axis=2,
    ).transpose(1, 0, 2)

    x = tokens.astype(f32)
    rstd = lax.rsqrt(jnp.mean(x * x, axis=-1, keepdims=True) + EPS)
    xhat = x * rstd
    n_full, weights = front(xhat.astype(bf16), pieces, 0)
    n_full = n_full.reshape(HALF_KEYS, 2048)
    weights = weights.reshape(2048, WIDTH)
    w_qkv = weights[:, :512]
    w_out = weights[:, 640:896]
    w_gate_up = weights[:, 896:2432]
    w_down = weights[:, 2432:]
    gain_q = weights[::16, 512].astype(f32)
    gain_k = weights[::16, 513].astype(f32)

    counts = seq_rows[0]
    position_all, segment = row_layout(counts, jnp.arange(16, dtype=jnp.int32)[:, None], ROWS)
    own_position = lax.dynamic_slice_in_dim(position_all.reshape(KEYS), yh * HALF_KEYS, HALF_KEYS)
    segment = jnp.tile(segment, 16)
    segment = jnp.where(segment < 0, 2 + jnp.arange(KEYS, dtype=jnp.int32), segment)
    own_segment = lax.dynamic_slice_in_dim(segment, yh * HALF_KEYS, HALF_KEYS)
    both_segments = jnp.stack([own_segment, segment[:HALF_KEYS]])
    late = yh.astype(jnp.int32).reshape(1)
    cosine, sine_part = rope_tables(own_position)

    c_full = gather_rows(cotangent, 1)
    projected = dot(n_full, w_qkv)

    def prepare_local(p, gq, gk):
        return prepare(p, gq, gk, cosine, sine_part)

    (q, k, v), prepare_back = jax.vjp(prepare_local, projected, gain_q, gain_k)
    q = q.astype(bf16).reshape(HALF_KEYS, 256)
    kv = jnp.concatenate([k.astype(bf16), v.astype(bf16)], axis=1)
    other_kv = lax.ppermute(kv, "yh", [(0, 1)])
    attended = attend(late, q, kv, other_kv, own_segment[:, None], both_segments)
    middle = x + scatter_rows(dot_nt(attended, w_out), 2)

    rstd_m = lax.rsqrt(jnp.mean(middle * middle, axis=-1, keepdims=True) + EPS)
    mhat = middle * rstd_m
    m_full = gather_rows(mhat.astype(bf16), 3)
    joined = dot(m_full, w_gate_up)
    hidden_f, swiglu_back = jax.vjp(swiglu, joined)
    hidden = hidden_f.astype(bf16)
    block_out = (middle + scatter_rows(dot_nt(hidden, w_down), 4)).astype(bf16)
    g_joined = swiglu_back(dot(c_full, w_down))[0].astype(bf16)
    g_mhat = scatter_rows(dot_nt(g_joined, w_gate_up), 5)
    g_middle = cotangent.astype(f32) + norm_back(g_mhat, mhat, rstd_m)
    down_part = dot_tn(c_full, hidden).astype(bf16)
    gate_up_part = dot_tn(m_full, g_joined).astype(bf16)

    b_full = gather_rows(g_middle.astype(bf16), 6)
    g_attended = dot(b_full, w_out).astype(bf16)
    out_part = dot_tn(b_full, attended).astype(bf16)
    g_q, g_kv, g_other_kv = attend_back(
        late, q, kv, other_kv, g_attended, own_segment[None], both_segments[:, :, None]
    )
    g_kv += lax.ppermute(g_other_kv.astype(bf16), "yh", [(1, 0)]).astype(f32)
    g_projected, g_gain_q, g_gain_k = prepare_back(
        (g_q.reshape(HALF_KEYS, 2, HEAD_SIZE), g_kv[:, :128], g_kv[:, 128:])
    )
    g_projected = g_projected.astype(bf16)
    g_xhat = scatter_rows(dot_nt(g_projected, w_qkv), 7)
    tokens_grad = g_middle + norm_back(g_xhat, xhat, rstd)
    qkv_part = dot_tn(n_full, g_projected).astype(bf16)
    gain_part = jnp.pad(
        jnp.stack([g_gain_q, g_gain_k], axis=1).astype(bf16)[:, None], ((0, 0), (0, 15), (0, 126))
    ).reshape(2048, 128)

    owned = scatter_grads(
        jnp.concatenate([qkv_part, gain_part, out_part, gate_up_part, down_part], axis=1), 8
    ).astype(f32)
    qkv_raw = unchunk(owned[:, :, :512], (256, 128, 128))
    gain_grads = jnp.sum(owned[:, 0, 512:514], axis=0)
    out_grad = unchunk(owned[:, :, 640:896], (256,))
    gate_up_raw = unchunk(owned[:, :, 896:2432], (768, 768))
    down_grad = unchunk(owned[:, :, 2432:], (768,))
    return (
        block_out,
        tokens_grad,
        qkv_raw * gain_a,
        out_grad,
        jnp.sum(qkv_raw * qkv_f, axis=1),
        gain_grads[:1],
        gain_grads[1:],
        gate_up_raw * gain_m,
        down_grad,
        jnp.sum(gate_up_raw * gate_up_f, axis=1),
    )


def solution(mesh):
    fine = Mesh(mesh.devices.reshape(4, 2, 2, 4, 2), AXES)
    rows2 = P(AXES, None)
    rows1 = P(AXES)
    return jax.shard_map(
        local,
        mesh=fine,
        in_specs=(
            rows2,
            rows2,
            P(("x", "yl"), None),
            rows2,
            rows2,
            rows1,
            rows1,
            rows1,
            rows2,
            rows2,
            rows1,
        ),
        out_specs=(
            rows2,
            rows2,
            rows2,
            rows2,
            rows1,
            rows1,
            rows1,
            rows2,
            rows2,
            rows1,
        ),
        check_vma=False,
    )
```

```python
import math

import jax
import jax.numpy as jnp
from jax import lax
from jax.experimental import pallas as pl
from jax.experimental.pallas import tpu as pltpu
from jax.sharding import Mesh
from jax.sharding import PartitionSpec as P

HEAD_SIZE = 128
FF = 6144
ROWS = 128
GROUP = 8
HALF_KEYS = ROWS * GROUP
KEYS = 2 * HALF_KEYS
SCALE = HEAD_SIZE**-0.5
WIDTH = 3200
EPS = 1e-6
ROPE_BASE = 1000000.0
AXES = ("x", "yl", "yh", "z", "c")
TP = ("z", "c")
PLANE = ("x", "yl", "yh")
f32 = jnp.float32
bf16 = jnp.bfloat16


def row_layout(seq_counts, device, token_rows):
    seq_ends = jnp.cumsum(seq_counts)
    starts = seq_ends - seq_counts
    row_place = jnp.arange(token_rows, dtype=jnp.int32)
    inside = (
        (row_place[:, None] >= starts[None, :]) & (row_place[:, None] < seq_ends[None, :])
    ).astype(jnp.int32)
    slot_ids = jnp.arange(seq_counts.shape[0], dtype=jnp.int32)
    in_sequence = row_place < seq_ends[-1]
    segment = jnp.where(in_sequence, jnp.sum(inside * slot_ids[None, :], axis=1), -1)
    length = jnp.sum(inside * seq_counts[None, :], axis=1)
    seq_begin = jnp.sum(inside * starts[None, :], axis=1)
    position = device * length[None, :] + row_place[None, :] - seq_begin[None, :]
    return (position, segment)


def dot(a, b):
    return jnp.dot(a, b, preferred_element_type=f32)


def dot_nt(a, b):
    return lax.dot_general(a, b, (((1,), (1,)), ((), ())), preferred_element_type=f32)


def dot_tn(a, b):
    return lax.dot_general(a, b, (((0,), (0,)), ((), ())), preferred_element_type=f32)


MESH = pl.DeviceIdType.MESH
ANY = pl.BlockSpec(memory_space=pl.ANY)
VM = pl.BlockSpec(memory_space=pltpu.VMEM)
SM = pl.BlockSpec(memory_space=pltpu.SMEM)
DMA = pltpu.SemaphoreType.DMA
HALF = 64
D = 2048
A_WIDTH = 896
B_WIDTH = 2304
LOG2E = 1.4426950408889634
scope = jax.named_scope


def params(cid=None, mib=56):
    if cid is None:
        return pltpu.CompilerParams(vmem_limit_bytes=mib << 20)
    return pltpu.CompilerParams(
        collective_id=cid, has_side_effects=True, vmem_limit_bytes=mib << 20
    )


def struct(shape, dtype):
    return jax.ShapeDtypeStruct(shape, dtype)


def rcopy(src, dst, send, recv, to):
    return pltpu.make_async_remote_copy(
        src, dst, send, recv, device_id=to, device_id_type=MESH
    )


def span(start, size, step=16):
    return pl.ds(pl.multiple_of(start, step), size)


def by_rows(rows, body, step=16):
    def run(i, carry):
        body(span(i * step, step, step))
        return carry

    lax.fori_loop(0, rows // step, run, 0)


def ring_place():
    z, c = lax.axis_index("z"), lax.axis_index("c")
    return z, c, lax.rem(z + 1, 4), lax.rem(z + 3, 4), lax.rem(z + 2, 4)


def plane_place():
    return lax.axis_index("x"), lax.axis_index("yh") * 2 + lax.axis_index("yl")


def y_slot(y):
    return lax.rem(y, 2) * 2 + y // 2


def slot(x, y):
    return x * 4 + y_slot(y)


def to_x(x):
    return {"x": x}


def to_y(y):
    return {"yl": lax.rem(y, 2), "yh": y // 2}


def to_group(j):
    return {"z": j // 2, "c": lax.rem(j, 2)}


def greet(targets):
    barrier = pltpu.get_barrier_semaphore()
    for to in targets:
        pl.semaphore_signal(barrier, inc=1, device_id=to, device_id_type=MESH)
    pl.semaphore_wait(barrier, len(targets))


def ring_targets():
    z, c, up, dn, far = ring_place()
    return [{"z": up}, {"z": dn}, {"c": 1 - c}]


def group_targets(me):
    return [to_group(lax.rem(me + d, GROUP)) for d in range(1, GROUP)]


def plane_targets(x, y):
    return [to_x(lax.rem(x + s, 4)) for s in (1, 2, 3)] + [
        to_y(lax.rem(y + s, 4)) for s in (1, 2, 3)
    ]


class RowGather:
    def __init__(self, src, dst, own_sem, send, recv):
        z, c, up, dn, far = ring_place()
        low, high = pl.ds(0, HALF), pl.ds(HALF, HALF)

        def at(zz, part=None):
            first = (2 * zz + c) * ROWS
            if part is None:
                return dst.at[span(first, ROWS)]
            return dst.at[span(first + part * HALF, HALF)]

        to_up, to_dn, to_sib = {"z": up}, {"z": dn}, {"c": 1 - c}
        plan = [
            (src.at[low], at(z, 0), to_up),
            (src.at[high], at(z, 1), to_up),
            (at(dn, 0), at(dn, 0), to_up),
            (src.at[high], at(z, 1), to_dn),
            (src.at[low], at(z, 0), to_dn),
            (at(up, 1), at(up, 1), to_dn),
            (src, at(z), to_sib),
            (at(dn), at(dn), to_sib),
            (at(up), at(up), to_sib),
            (at(far, 0), at(far, 0), to_sib),
            (at(far, 1), at(far, 1), to_sib),
        ]
        self.cp = [rcopy(a, b, send.at[i], recv.at[i], to) for i, (a, b, to) in enumerate(plan)]
        self.own = pltpu.make_async_copy(src, at(z), own_sem)

    def start(self):
        self.own.start()
        for i in (0, 3, 1, 4, 6):
            self.cp[i].start()

    def relay(self):
        cp = self.cp
        cp[0].wait_recv()
        cp[2].start()
        cp[3].wait_recv()
        cp[5].start()

    def share(self):
        cp = self.cp
        cp[1].wait_recv()
        cp[7].start()
        cp[4].wait_recv()
        cp[8].start()

    def have_own(self):
        self.own.wait()
        self.cp[6].wait_recv()

    def have_dn(self):
        self.cp[7].wait_recv()

    def have_up(self):
        self.cp[8].wait_recv()

    def share_far(self):
        cp = self.cp
        cp[2].wait_recv()
        cp[9].start()
        cp[5].wait_recv()
        cp[10].start()

    def have_far(self):
        self.cp[9].wait_recv()
        self.cp[10].wait_recv()

    def drain(self):
        for c in self.cp:
            c.wait_send()


GATHER_SCRATCH = [DMA((1,)), DMA((11,)), DMA((11,))]


def scatter_scratch(n=D):
    return [
        pltpu.VMEM((4, ROWS, n), bf16),
        pltpu.VMEM((3, ROWS, n), bf16),
        pltpu.VMEM((2, ROWS, n), bf16),
        pltpu.VMEM((2, HALF, n), bf16),
        DMA((10,)),
        DMA((10,)),
    ]


class RowScatter:
    def __init__(self, p, sib_in, acc, near, fwd, send, recv):
        z, c, up, dn, far = ring_place()
        self.order = (far, up, dn, z)
        self.p, self.sib_in, self.acc, self.near, self.fwd, self.c = p, sib_in, acc, near, fwd, c
        low, high = pl.ds(0, HALF), pl.ds(HALF, HALF)
        to_up, to_dn, to_sib = {"z": up}, {"z": dn}, {"c": 1 - c}
        self.sib = [
            rcopy(
                p.at[span((2 * zz + 1 - c) * ROWS, ROWS)],
                sib_in.at[k],
                send.at[k],
                recv.at[k],
                to_sib,
            )
            for k, zz in enumerate(self.order)
        ]
        plan = [
            (acc.at[0, low], fwd.at[0], to_dn),
            (acc.at[0, high], fwd.at[1], to_up),
            (acc.at[1, low], near.at[1, low], to_up),
            (acc.at[1, high], near.at[1, high], to_up),
            (acc.at[2, high], near.at[0, high], to_dn),
            (acc.at[2, low], near.at[0, low], to_dn),
        ]
        self.cp = [
            rcopy(a, b, send.at[4 + i], recv.at[4 + i], to) for i, (a, b, to) in enumerate(plan)
        ]

    def swap(self, k):
        self.sib[k].start()

    def add(self, k):
        self.sib[k].wait_recv()
        first = (2 * self.order[k] + self.c) * ROWS

        def body(r):
            mine = self.p[span(first + r.start, 16)].astype(f32)
            self.acc[k, r] = (mine + self.sib_in[k, r].astype(f32)).astype(bf16)

        by_rows(ROWS, body)
        if k == 0:
            self.cp[0].start()
            self.cp[1].start()
        else:
            self.cp[2 * k].start()

    def relay(self):
        for arrive, k, part, then in ((1, 1, 1, 3), (0, 2, 0, 5)):
            self.cp[arrive].wait_recv()

            def body(r):
                at = span(part * HALF + r.start, 16)
                t = self.acc[k, at].astype(f32) + self.fwd[part, r].astype(f32)
                self.acc[k, at] = t.astype(bf16)

            by_rows(HALF, body)
            self.cp[then].start()

    def finish(self, body):
        self.sib[3].wait_recv()
        for i in (2, 3, 4, 5):
            self.cp[i].wait_recv()
        first = (2 * self.order[3] + self.c) * ROWS

        def run(r):
            t = self.p[span(first + r.start, 16)].astype(f32) + self.sib_in[3, r].astype(f32)
            t += self.near[0, r].astype(f32) + self.near[1, r].astype(f32)
            body(r, t)

        by_rows(ROWS, run)
        for s in self.sib + self.cp:
            s.wait_send()


class Ring:
    def __init__(self, axis, at, block, first, rows, send, recv):
        step = to_x if axis == "x" else to_y
        up, dn = lax.rem(at + 1, 4), lax.rem(at + 3, 4)

        def part(who, start, size):
            return block[0].at[span(block[1](who) * ROWS + start, size)]

        half = rows // 2
        plan = [
            (part(at, first, rows), step(up)),
            (part(at, first, rows), step(dn)),
            (part(dn, first, half), step(up)),
            (part(up, first + half, half), step(dn)),
        ]
        self.cp = [rcopy(r, r, send.at[i], recv.at[i], to) for i, (r, to) in enumerate(plan)]

    def start(self):
        self.cp[0].start()
        self.cp[1].start()

    def relay(self):
        self.cp[0].wait_recv()
        self.cp[2].start()
        self.cp[1].wait_recv()
        self.cp[3].start()

    def finish(self):
        self.cp[2].wait_recv()
        self.cp[3].wait_recv()

    def drain(self):
        for c in self.cp:
            c.wait_send()


class PlaneGather:
    def __init__(self, dst, send, recv):
        x, y = plane_place()
        self.halves = []
        for half in (0, 1):

            def ring(axis, other, k):
                if axis == "x":
                    block, at = (dst, lambda who: slot(who, other)), x
                else:
                    block, at = (dst, lambda who: slot(other, who)), y
                return Ring(axis, at, block, half * HALF, HALF, send.at[half, k], recv.at[half, k])

            axes = ("y", "x") if half == 0 else ("x", "y")
            here, over = (y, x) if half == 0 else (x, y)
            others = [here, lax.rem(here + 3, 4), lax.rem(here + 1, 4), lax.rem(here + 2, 4)]
            self.halves.append(
                [ring(axes[0], over, 0)] + [ring(axes[1], o, 1 + k) for k, o in enumerate(others)]
            )

    def both(self, k, what):
        for half in self.halves:
            getattr(half[k], what)()

    def one(self):
        self.both(0, "start")
        self.both(1, "start")

    def two(self):
        self.both(0, "relay")
        self.both(2, "start")
        self.both(3, "start")

    def three(self):
        self.both(1, "relay")
        self.both(0, "finish")
        self.both(4, "start")

    def four(self):
        self.both(2, "relay")
        self.both(3, "relay")

    def five(self):
        self.both(4, "relay")

    def finish(self):
        for k in range(1, 5):
            self.both(k, "finish")
        for k in range(5):
            self.both(k, "drain")


PLANE_SCRATCH = [DMA((2, 5, 4)), DMA((2, 5, 4))]


class GroupSwap:
    def __init__(self, src, dst, own_sem, send, recv):
        z, c, up, dn, far = ring_place()
        me = 2 * z + c
        self.own = pltpu.make_async_copy(src(me), dst(me), own_sem)
        self.cp = []
        for d in range(1, GROUP):
            j = lax.rem(me + d, GROUP)
            self.cp.append(rcopy(src(j), dst(me), send.at[d - 1], recv.at[d - 1], to_group(j)))

    def start(self):
        self.own.start()
        for s in self.cp:
            s.start()

    def finish(self):
        self.own.wait()
        for s in self.cp:
            s.wait_recv()

    def drain(self):
        for s in self.cp:
            s.wait_send()


SWAP_SCRATCH = [DMA((1,)), DMA((7,)), DMA((7,))]


def turn(values):
    return pltpu.roll(values, 64, 1)


def front_kernel(
    tok_ref, qkv_ref, out_ref, gu_ref, dw_ref, ga_ref, gm_ref, hg_ref, pos_ref,
    n_out, wa_out, b_ref, proj_ref, q_ref, kv_ref, gains_ref, tab_ref,
    xh, pa, pb, n, wa, store_sems,
    g_own, g_send, g_recv, sa_own, sa_send, sa_recv, sb_own, sb_send, sb_recv, w_send, w_recv,
):
    z, c, up, dn, far = ring_place()
    me = 2 * z + c
    x, y = plane_place()

    def norm(r):
        t = tok_ref[r].astype(f32)
        xh[r] = (t * lax.rsqrt(jnp.mean(t * t, axis=-1, keepdims=True) + EPS)).astype(bf16)

    by_rows(ROWS, norm)
    ga, gm = ga_ref[...].astype(f32), gm_ref[...].astype(f32)
    for j in range(GROUP):
        pa[j, :, 0:256] = (qkv_ref[:, 256 * j : 256 * j + 256].astype(f32) * ga).astype(bf16)
        for k in range(2):
            first = 2048 + 1024 * k + 128 * j
            pa[j, :, 256 + 128 * k : 384 + 128 * k] = (
                qkv_ref[:, first : first + 128].astype(f32) * ga
            ).astype(bf16)
        pa[j, :, 512:640] = jnp.broadcast_to(hg_ref[...], (16, 128))
        pa[j, :, 640:896] = out_ref[:, 256 * j : 256 * j + 256]
        for k in range(2):
            first = 6144 * k + 768 * j
            pb[j, :, 768 * k : 768 * k + 768] = (
                gu_ref[:, first : first + 768].astype(f32) * gm
            ).astype(bf16)
        pb[j, :, 1536:2304] = dw_ref[:, 768 * j : 768 * j + 768]

    with scope("front_greet"):
        greet(group_targets(me) + plane_targets(x, y))
    own_slot = slot(x, y) * ROWS
    swap_a = GroupSwap(
        lambda j: pa.at[j], lambda j: wa.at[span(own_slot + 16 * j, 16)], sa_own.at[0], sa_send, sa_recv
    )
    swap_b = GroupSwap(lambda j: pb.at[j], lambda j: b_ref.at[span(16 * j, 16)], sb_own.at[0], sb_send, sb_recv)
    gather = RowGather(xh, n, g_own.at[0], g_send, g_recv)
    plane = PlaneGather(wa, w_send, w_recv)
    swap_a.start()
    gather.start()
    with scope("front_swap"):
        swap_a.finish()
    plane.one()

    lane = lax.broadcasted_iota(jnp.int32, (1, 128), 1)
    k = lax.rem(lane, 64).astype(f32)
    freq = jnp.exp(k * (-2.0 * math.log(ROPE_BASE) / HEAD_SIZE))
    sign = jnp.where(lane < 64, -1.0, 1.0)

    def table(r):
        angle = pos_ref[r, :] * freq
        tab_ref[0, r] = jnp.cos(angle)
        tab_ref[1, r] = jnp.sin(angle) * sign

    with scope("front_table"):
        by_rows(HALF_KEYS, table, 64)
    with scope("front_relay"):
        gather.relay()
    with scope("front_two"):
        plane.two()
    with scope("front_three"):
        plane.three()
    with scope("front_share"):
        gather.share()
    swap_b.start()
    with scope("front_four"):
        plane.four()
    with scope("front_five"):
        plane.five()
    with scope("front_plane"):
        plane.finish()
    store_w = pltpu.make_async_copy(wa, wa_out, store_sems.at[1])
    store_w.start()

    with scope("front_gains"):
        row = lax.broadcasted_iota(jnp.int32, (D, 128), 0)
        col = lax.broadcasted_iota(jnp.int32, (D, 128), 1)
        pick = (row == 16 * col).astype(bf16)
        gains = dot_tn(wa[:, 512:640], pick)[0:8]
        gains_ref[...] = gains

    def project(zz):
        rows = span(256 * zz, 256, 256)
        proj_ref[rows, :] = dot(n[rows, :], wa[:, 0:512])

        def shape(r):
            r = span(256 * zz + r.start, 64, 64)
            for h in range(3):
                v = proj_ref[r, 128 * h : 128 * h + 128]
                g = gains[0:1] if h < 2 else gains[1:2]
                u = v * lax.rsqrt(jnp.mean(v * v, axis=-1, keepdims=True) + EPS) * g
                o = (u * tab_ref[0, r] + turn(u) * tab_ref[1, r]).astype(bf16)
                if h < 2:
                    q_ref[r, 128 * h : 128 * h + 128] = o
                else:
                    kv_ref[r, 0:128] = o
            kv_ref[r, 128:256] = proj_ref[r, 384:512].astype(bf16)

        by_rows(256, shape, 64)

    with scope("front_own"):
        gather.have_own()
        project(z)
    with scope("front_dn"):
        gather.have_dn()
        project(dn)
    with scope("front_share_far"):
        gather.share_far()
    with scope("front_up"):
        gather.have_up()
        project(up)
    with scope("front_have_far"):
        gather.have_far()
    store_n = pltpu.make_async_copy(n, n_out, store_sems.at[0])
    store_n.start()
    with scope("front_far"):
        project(far)
    with scope("front_end"):
        swap_b.finish()
        gather.drain()
        swap_a.drain()
        swap_b.drain()
        store_n.wait()
        store_w.wait()


def front(tokens, qkv, out, gu, dw, ga, gm, hg, pos, cid):
    return pl.pallas_call(
        front_kernel,
        out_shape=(
            struct((HALF_KEYS, D), bf16),
            struct((D, A_WIDTH), bf16),
            struct((ROWS, B_WIDTH), bf16),
            struct((HALF_KEYS, 512), f32),
            struct((HALF_KEYS, 256), bf16),
            struct((HALF_KEYS, 256), bf16),
            struct((8, 128), f32),
            struct((2, HALF_KEYS, 128), f32),
        ),
        in_specs=[VM] * 9,
        out_specs=(ANY, ANY, ANY, VM, VM, VM, VM, VM),
        scratch_shapes=[
            pltpu.VMEM((ROWS, D), bf16),
            pltpu.VMEM((GROUP, 16, A_WIDTH), bf16),
            pltpu.VMEM((GROUP, 16, B_WIDTH), bf16),
            pltpu.VMEM((HALF_KEYS, D), bf16),
            pltpu.VMEM((D, A_WIDTH), bf16),
            DMA((2,)),
        ]
        + GATHER_SCRATCH
        + SWAP_SCRATCH
        + SWAP_SCRATCH
        + PLANE_SCRATCH,
        compiler_params=params(cid),
        name="front",
    )(tokens, qkv, out, gu, dw, ga, gm, hg, pos)


def weigh(q, keys, values, ok):
    p = jnp.where(ok, jnp.exp2(dot_nt(q, keys) * (SCALE * LOG2E)), 0.0)
    return jnp.sum(p, axis=1, keepdims=True), dot(p.astype(bf16), values)


def attend_kernel(
    q_ref, kv_ref, qseg_ref, kseg_ref, b_ref, cot_ref, wa_ref, tok_ref,
    wb_ref, c_ref, okv_ref, att_ref, mid_ref, mhat_ref,
    acc, tot, wo, p, sems, kv_sems,
    g_own, g_send, g_recv, w_send, w_recv, sib_in, s_acc, near, fwd, r_send, r_recv,
):
    x, y = plane_place()
    yh = lax.axis_index("yh")
    with scope("attend_greet"):
        greet(ring_targets() + plane_targets(x, y))
    own = pltpu.make_async_copy(b_ref, wb_ref.at[span(slot(x, y) * ROWS, ROWS)], sems.at[0])
    own.start()
    get_wo = pltpu.make_async_copy(wa_ref.at[:, pl.ds(640, 256)], wo, sems.at[1])
    get_wo.start()
    gather = RowGather(cot_ref, c_ref, g_own.at[0], g_send, g_recv)
    plane = PlaneGather(wb_ref, w_send, w_recv)
    scatter = RowScatter(p, sib_in, s_acc, near, fwd, r_send, r_recv)
    give_kv = rcopy(kv_ref, okv_ref, kv_sems.at[0], kv_sems.at[1], {"yh": 1 - yh})

    @pl.when(yh == 0)
    def _():
        give_kv.start()
        okv_ref[...] = jnp.zeros_like(okv_ref)

    gather.start()
    own.wait()
    plane.one()

    def near_keys(h):
        cols = pl.ds(128 * h, 128)
        for i in range(4):
            rows = pl.ds(256 * i, 256)
            q = q_ref[rows, cols]
            t = jnp.zeros((256, 1), f32)
            a = jnp.zeros((256, 128), f32)
            for k in range(i + 1):
                keys = pl.ds(256 * k, 256)
                ok = qseg_ref[rows, :] == kseg_ref[0:1, keys]
                if k == i:
                    ok &= lax.broadcasted_iota(jnp.int32, (256, 256), 0) >= lax.broadcasted_iota(
                        jnp.int32, (256, 256), 1
                    )
                dt, da = weigh(q, kv_ref[keys, 0:128], kv_ref[keys, 128:256], ok)
                t += dt
                a += da
            acc[rows, cols] = a
            tot[h, rows] = t

    def far_keys(h):
        cols = pl.ds(128 * h, 128)

        def body(i, carry):
            rows = span(256 * i, 256, 256)
            q = q_ref[rows, cols]
            t = tot[h, rows]
            a = acc[rows, cols]
            for k in range(4):
                keys = pl.ds(256 * k, 256)
                ok = qseg_ref[rows, :] == kseg_ref[1:2, keys]
                dt, da = weigh(q, okv_ref[keys, 0:128], okv_ref[keys, 128:256], ok)
                t += dt
                a += da
            tot[h, rows] = t
            acc[rows, cols] = a
            return carry

        lax.fori_loop(0, 4, body, 0)

    with scope("attend_near0"):
        near_keys(0)
    with scope("attend_relay"):
        gather.relay()
    with scope("attend_near1"):
        near_keys(1)
    with scope("attend_two"):
        plane.two()
    with scope("attend_share"):
        gather.share()

    @pl.when(yh == 1)
    def _():
        with scope("attend_kv"):
            give_kv.wait_recv()
        with scope("attend_far_keys"):
            far_keys(0)
            far_keys(1)

    @pl.when(yh == 0)
    def _():
        give_kv.wait_send()

    with scope("attend_norm"):
        for h in range(2):
            cols = pl.ds(128 * h, 128)
            att_ref[:, cols] = (acc[:, cols] / tot[h]).astype(bf16)
        get_wo.wait()
    for k, zz in enumerate(scatter.order):
        rows = span(256 * zz, 256, 256)
        with scope("attend_out"):
            for n in range(4):
                cols = pl.ds(512 * n, 512)
                p[rows, cols] = dot_nt(att_ref[rows, :], wo[cols, :]).astype(bf16)
        scatter.swap(k)
        if k:
            with scope("attend_add"):
                scatter.add(k - 1)
    with scope("attend_three"):
        plane.three()
    with scope("attend_share_far"):
        gather.share_far()
    with scope("attend_scatter_relay"):
        scatter.relay()
    with scope("attend_four"):
        plane.four()
    with scope("attend_gather"):
        gather.have_own()
        gather.have_dn()
        gather.have_up()
        gather.have_far()

    def close(r, t):
        m = tok_ref[r].astype(f32) + t
        mid_ref[r] = m
        mhat_ref[r] = (m * lax.rsqrt(jnp.mean(m * m, axis=-1, keepdims=True) + EPS)).astype(bf16)

    with scope("attend_scatter_end"):
        scatter.finish(close)
    with scope("attend_five"):
        plane.five()
    with scope("attend_end"):
        gather.drain()
        plane.finish()


def attend(q, kv, qseg, kseg, b, cot, wa, tokens, cid):
    return pl.pallas_call(
        attend_kernel,
        out_shape=(
            struct((D, B_WIDTH), bf16),
            struct((HALF_KEYS, D), bf16),
            struct((HALF_KEYS, 256), bf16),
            struct((HALF_KEYS, 256), bf16),
            struct((ROWS, D), f32),
            struct((ROWS, D), bf16),
        ),
        in_specs=[VM, VM, VM, VM, ANY, ANY, ANY, VM],
        out_specs=(ANY, ANY, VM, VM, VM, VM),
        scratch_shapes=[
            pltpu.VMEM((HALF_KEYS, 256), f32),
            pltpu.VMEM((2, HALF_KEYS, 1), f32),
            pltpu.VMEM((D, 256), bf16),
            pltpu.VMEM((HALF_KEYS, D), bf16),
            DMA((2,)),
            DMA((2,)),
        ]
        + GATHER_SCRATCH
        + PLANE_SCRATCH
        + scatter_scratch(),
        compiler_params=params(cid),
        name="attend",
    )(q, kv, qseg, kseg, b, cot, wa, tokens)


def mlp_kernel(
    mhat_ref, mid_ref, cot_ref, c_ref, wb_ref,
    hid_ref, gmid_ref, gbr_ref, grad_ref,
    m, cb, wb, gj, p, stage, sems, stage_sems,
    g_own, g_send, g_recv, sib_in, s_acc, near, fwd, r_send, r_recv,
):
    z, c, up, dn, far = ring_place()
    get_w = pltpu.make_async_copy(wb_ref, wb, sems.at[0])
    get_c = pltpu.make_async_copy(c_ref, cb, sems.at[1])
    get_w.start()
    get_c.start()
    greet(ring_targets())
    gather = RowGather(mhat_ref, m, g_own.at[0], g_send, g_recv)
    scatter = RowScatter(p, sib_in, s_acc, near, fwd, r_send, r_recv)
    gather.start()
    gather.have_own()
    with scope("mlp_get"):
        get_w.wait()
        get_c.wait()

    def block(zz):
        rows = span(256 * zz, 256, 256)
        for t in range(3):
            gate_cols, up_cols = pl.ds(256 * t, 256), pl.ds(768 + 256 * t, 256)
            gate = dot(m[rows, :], wb[:, gate_cols])
            upper = dot(m[rows, :], wb[:, up_cols])
            gh = dot(cb[rows, :], wb[:, 1536 + 256 * t : 1792 + 256 * t])
            sig = 1.0 / (1.0 + jnp.exp(-gate))
            act = gate * sig
            hid_ref[rows, gate_cols] = (act * upper).astype(bf16)
            gj[rows, up_cols] = (gh * act).astype(bf16)
            gj[rows, gate_cols] = (gh * upper * (sig + act * (1.0 - sig))).astype(bf16)

    def back(zz):
        rows = span(256 * zz, 256, 256)
        for n in range(4):
            cols = pl.ds(512 * n, 512)
            p[rows, cols] = dot_nt(gj[rows, :], wb[cols, 0:1536]).astype(bf16)

    with scope("mlp_own"):
        block(z)
    with scope("mlp_relay"):
        gather.relay()
    with scope("mlp_own_back"):
        back(z)
    scatter.swap(3)
    with scope("mlp_share"):
        gather.share()
        gather.have_dn()
    with scope("mlp_dn"):
        block(dn)
        back(dn)
    scatter.swap(2)
    with scope("mlp_share_far"):
        gather.share_far()
        gather.have_up()
    with scope("mlp_up"):
        block(up)
        back(up)
    with scope("mlp_add"):
        scatter.add(2)
    scatter.swap(1)
    with scope("mlp_have_far"):
        gather.have_far()
    with scope("mlp_far"):
        block(far)
        back(far)
    scatter.swap(0)
    with scope("mlp_adds"):
        scatter.add(1)
        scatter.add(0)

    def put(i):
        return pltpu.make_async_copy(
            stage.at[lax.rem(i, 2)], grad_ref.at[span(256 * i, 256, 256)], stage_sems.at[lax.rem(i, 2)]
        )

    def grads(i, carry):
        @pl.when(i >= 2)
        def _():
            put(i - 2).wait()

        cols = span(256 * i, 256, 256)
        s = lax.rem(i, 2)
        for n in range(3):
            part = pl.ds(512 * n, 512)
            stage[s, :, part] = dot_tn(m[:, cols], gj[:, part]).astype(bf16)
        stage[s, :, 1536:2304] = dot_tn(cb[:, cols], hid_ref[...]).astype(bf16)
        put(i).start()
        return carry

    with scope("mlp_grads"):
        lax.fori_loop(0, 4, grads, 0)
    with scope("mlp_scatter_relay"):
        scatter.relay()
    with scope("mlp_grads2"):
        lax.fori_loop(4, 8, grads, 0)

    def close(r, t):
        v = mid_ref[r]
        s = lax.rsqrt(jnp.mean(v * v, axis=-1, keepdims=True) + EPS)
        hat = v * s
        g = cot_ref[r].astype(f32) + s * (t - hat * jnp.mean(t * hat, axis=-1, keepdims=True))
        gmid_ref[r] = g
        gbr_ref[r] = g.astype(bf16)

    with scope("mlp_scatter_end"):
        scatter.finish(close)
    with scope("mlp_end"):
        gather.drain()
        put(6).wait()
        put(7).wait()


def mlp(mhat, middle, cot, c_full, wb, cid):
    return pl.pallas_call(
        mlp_kernel,
        out_shape=(
            struct((HALF_KEYS, 768), bf16),
            struct((ROWS, D), f32),
            struct((ROWS, D), bf16),
            struct((D, B_WIDTH), bf16),
        ),
        in_specs=[VM, VM, VM, ANY, ANY],
        out_specs=(VM, VM, VM, ANY),
        scratch_shapes=[
            pltpu.VMEM((HALF_KEYS, D), bf16),
            pltpu.VMEM((HALF_KEYS, D), bf16),
            pltpu.VMEM((D, B_WIDTH), bf16),
            pltpu.VMEM((HALF_KEYS, 1536), bf16),
            pltpu.VMEM((HALF_KEYS, D), bf16),
            pltpu.VMEM((2, 256, B_WIDTH), bf16),
            DMA((2,)),
            DMA((2,)),
        ]
        + GATHER_SCRATCH
        + scatter_scratch(),
        compiler_params=params(cid, 60),
        name="mlp",
    )(mhat, middle, cot, c_full, wb)


class RingSum:
    def __init__(self, step, at, src, own, fwd, near, rel, send, recv, load, lead):
        up, dn, far = lax.rem(at + 1, 4), lax.rem(at + 3, 4), lax.rem(at + 2, 4)
        n = 4 if lead else HALF
        lo, hi = pl.ds(0, n // 2), pl.ds(n // 2, n // 2)
        self.lead, self.half = lead, n // 2
        self.own, self.fwd, self.near, self.rel = own, fwd, near, rel
        plan = [
            (src(far).at[lo], fwd.at[0], step(dn)),
            (src(far).at[hi], fwd.at[1], step(up)),
            (src(up).at[lo], near.at[1, lo], step(up)),
            (rel.at[1], near.at[1, hi], step(up)),
            (src(dn).at[hi], near.at[0, hi], step(dn)),
            (rel.at[0], near.at[0, lo], step(dn)),
        ]
        self.cp = [rcopy(a, b, send.at[i], recv.at[i], to) for i, (a, b, to) in enumerate(plan)]
        self.loads = [
            pltpu.make_async_copy(a, b, load.at[i])
            for i, (a, b) in enumerate(
                [(src(at), own), (src(dn).at[lo], rel.at[0]), (src(up).at[hi], rel.at[1])]
            )
        ]

    def start(self):
        for i in (0, 1, 2, 4):
            self.cp[i].start()
        for c in self.loads:
            c.start()

    def tiles(self, whole, body):
        if self.lead:
            count = 16 if whole else 8

            def run(i, carry):
                body((i // 4, span(lax.rem(i, 4) * 16, 16)))
                return carry
        else:
            count = 4 if whole else 2

            def run(i, carry):
                body((span(i * 16, 16),))
                return carry

        lax.fori_loop(0, count, run, 0)

    def relay(self):
        for k, arrive, then in ((1, 1, 3), (0, 0, 5)):
            self.cp[arrive].wait_recv()
            self.loads[1 + k].wait()

            def body(at):
                t = self.rel[(k, *at)].astype(f32) + self.fwd[(k, *at)].astype(f32)
                self.rel[(k, *at)] = t.astype(bf16)

            self.tiles(False, body)
            self.cp[then].start()

    def finish(self):
        self.loads[0].wait()
        for i in (2, 3, 4, 5):
            self.cp[i].wait_recv()

        def body(at):
            t = self.own[at].astype(f32) + self.near[(0, *at)].astype(f32)
            self.own[at] = (t + self.near[(1, *at)].astype(f32)).astype(bf16)

        self.tiles(True, body)

    def drain(self):
        for c in self.cp:
            c.wait_send()


def plane_scatter_scratch(w):
    first = [pltpu.VMEM((4, HALF, w), bf16), pltpu.VMEM((2, 2, HALF, w), bf16), pltpu.VMEM((2, 4, HALF, w), bf16), pltpu.VMEM((2, 2, HALF, w), bf16)]
    second = [pltpu.VMEM((2, HALF // 2, w), bf16), pltpu.VMEM((2, HALF, w), bf16), pltpu.VMEM((2, HALF // 2, w), bf16)]
    return first * 2 + second * 2 + [pltpu.VMEM((ROWS, w), bf16), DMA((4, 6)), DMA((4, 6)), DMA((4, 3))]


PLANE_SCATTER = 18


class PlaneScatter:
    def __init__(self, src, buffers):
        x, y = plane_place()
        a1, b1, a2, b2 = buffers[0:4], buffers[4:8], buffers[8:11], buffers[11:14]
        self.last, send, recv, load = buffers[14:18]
        low, high = pl.ds(0, HALF), pl.ds(HALF, HALF)

        def ring(i, step, at, block, own, rest):
            return RingSum(step, at, block, own, *rest, send.at[i], recv.at[i], load.at[i], i < 2)

        own_a, own_b = a1[0], b1[0]
        self.first = [
            ring(0, to_x, x, lambda k: src.at[k, :, low], own_a, a1[1:]),
            ring(1, to_y, y, lambda k: src.at[:, y_slot(k), high], own_b, b1[1:]),
        ]
        self.second = [
            ring(2, to_y, y, lambda k: own_a.at[y_slot(k)], self.last.at[low], a2),
            ring(3, to_x, x, lambda k: own_b.at[k], self.last.at[high], b2),
        ]

    def start(self):
        for r in self.first:
            r.start()

    def relay(self):
        for r in self.first:
            r.relay()

    def turn(self):
        for r, s in zip(self.first, self.second):
            r.finish()
            s.start()

    def relay2(self):
        for r in self.second:
            r.relay()

    def finish(self):
        for r in self.second:
            r.finish()

    def drain(self):
        for r in self.first + self.second:
            r.drain()


def swap_last(last, out, own, send, recv):
    return GroupSwap(lambda j: last.at[span(16 * j, 16)], lambda j: out.at[j], own.at[0], send, recv)


def back_kernel(
    gbr_ref, wa_ref, wb_ref, att_ref, q_ref, kv_ref, okv_ref, qseg_ref, kseg_ref, hid_ref, mid_ref,
    proj_ref, tab_ref, gains_ref, part_ref,
    bo_ref, gp_ref, gsum_ref, outp_ref, owned_ref,
    g, wo, wd, p, gatt, ps, gps, tot, inn, gq, gkv, gokv, give, take, sems, kv_sems, *rest,
):
    g_own, g_send, g_recv, sib_in, s_acc, near, fwd, r_send, r_recv = rest[:9]
    buffers, (s_own, s_send, s_recv) = rest[9 : 9 + PLANE_SCATTER], rest[9 + PLANE_SCATTER :]
    z, c, up, dn, far = ring_place()
    x, y = plane_place()
    yh = lax.axis_index("yh")
    get_wo = pltpu.make_async_copy(wa_ref.at[:, pl.ds(640, 256)], wo, sems.at[0])
    get_wd = pltpu.make_async_copy(wb_ref.at[:, pl.ds(1536, 768)], wd, sems.at[1])
    get_wd.start()
    get_wo.start()
    greet(group_targets(2 * z + c) + plane_targets(x, y))
    gather = RowGather(gbr_ref, g, g_own.at[0], g_send, g_recv)
    scatter = RowScatter(p, sib_in, s_acc, near, fwd, r_send, r_recv)
    planes = PlaneScatter(part_ref, buffers)
    swap = swap_last(planes.last, owned_ref, s_own, s_send, s_recv)
    give_kv = rcopy(give, take, kv_sems.at[0], kv_sems.at[1], {"yh": 1 - yh})
    gather.start()
    planes.start()
    gkv[...] = jnp.zeros_like(gkv)
    gokv[...] = jnp.zeros_like(gokv)
    gq[...] = jnp.zeros_like(gq)
    gsum_ref[...] = jnp.zeros_like(gsum_ref)
    get_wd.wait()

    def down(k):
        rows = span(256 * scatter.order[k], 256, 256)
        for n in range(4):
            cols = pl.ds(512 * n, 512)
            p[rows, cols] = dot_nt(hid_ref[rows, :], wd[cols, :]).astype(bf16)
        scatter.swap(k)

    down(0)
    down(1)
    gather.relay()
    down(2)
    down(3)
    get_wo.wait()
    gather.share()

    def attended_grad(zz):
        rows = span(256 * zz, 256, 256)
        gatt[rows, :] = dot(g[rows, :], wo[...]).astype(bf16)

    gather.have_own()
    attended_grad(z)
    gather.have_dn()
    attended_grad(dn)
    gather.have_up()
    attended_grad(up)
    gather.share_far()
    scatter.add(0)
    scatter.add(1)
    scatter.add(2)
    gather.have_far()
    attended_grad(far)

    def weigh_back(i, h, which, k, diagonal):
        rows, cols = pl.ds(256 * i, 256), pl.ds(128 * h, 128)
        source = okv_ref if which else kv_ref
        keys, at = span(256 * k, 256, 256), span(256 * k + 1024 * which, 256, 256)
        s = dot_nt(source[keys, 0:128], q_ref[rows, cols])
        ok = kseg_ref[which, keys] == qseg_ref[0:1, rows]
        if diagonal:
            ok &= lax.broadcasted_iota(jnp.int32, (256, 256), 1) >= lax.broadcasted_iota(
                jnp.int32, (256, 256), 0
            )
        w = jnp.where(ok, jnp.exp2(s * (SCALE * LOG2E)), 0.0)
        gw = dot_nt(source[keys, 128:256], gatt[rows, cols])
        tot[...] += jnp.sum(w, axis=0, keepdims=True)
        inn[...] += jnp.sum(w * gw, axis=0, keepdims=True)
        ps[at] = w
        gps[at] = gw

    def spread(i, h, which, k):
        rows, cols = pl.ds(256 * i, 256), pl.ds(128 * h, 128)
        source, out = (okv_ref, gokv) if which else (kv_ref, gkv)
        keys, at = span(256 * k, 256, 256), span(256 * k + 1024 * which, 256, 256)
        w = ps[at] * tot[...]
        ds = (w * (gps[at] - inn[...]) * SCALE).astype(bf16)
        out[keys, 0:128] += dot(ds, q_ref[rows, cols])
        out[keys, 128:256] += dot(w.astype(bf16), gatt[rows, cols])
        gq[rows, cols] += dot_tn(ds, source[keys, 0:128])

    def attention(i, h):
        tot[...] = jnp.zeros_like(tot)
        inn[...] = jnp.zeros_like(inn)

        @pl.when(yh == 1)
        def _():
            def body(k, carry):
                weigh_back(i, h, 1, k, False)
                return carry

            lax.fori_loop(0, 4, body, 0)

        for k in range(i + 1):
            weigh_back(i, h, 0, k, k == i)
        inv = 1.0 / tot[...]
        tot[...] = inv
        inn[...] = inn[...] * inv

        @pl.when(yh == 1)
        def _():
            def body(k, carry):
                spread(i, h, 1, k)
                return carry

            lax.fori_loop(0, 4, body, 0)

        for k in range(i + 1):
            spread(i, h, 0, k)

    for i in range(4):
        attention(i, 0)
        attention(i, 1)
        if i == 1:
            planes.relay()
        if i == 2:
            scatter.relay()

    @pl.when(yh == 1)
    def _():
        def body(r):
            give[r] = gokv[r].astype(bf16)

        by_rows(HALF_KEYS, body, 64)
        give_kv.start()

    def back_head(r, h, grad):
        v = proj_ref[r, 128 * h : 128 * h + 128]
        k = h // 2
        scale = lax.rsqrt(jnp.mean(v * v, axis=-1, keepdims=True) + EPS)
        hat = v * scale
        du = grad * tab_ref[0, r] + turn(grad * tab_ref[1, r])
        gsum_ref[k : k + 1] += jnp.sum(du * hat, axis=0, keepdims=True)
        dh = du * gains_ref[k : k + 1]
        dv = scale * (dh - hat * jnp.mean(dh * hat, axis=-1, keepdims=True))
        gp_ref[r, 128 * h : 128 * h + 128] = dv.astype(bf16)

    def back_query(r):
        for h in range(2):
            back_head(r, h, gq[r, 128 * h : 128 * h + 128])

    by_rows(HALF_KEYS, back_query, 64)

    def close(r, t):
        bo_ref[r] = (mid_ref[r] + t).astype(bf16)

    scatter.finish(close)
    for n in range(8):
        cols = pl.ds(256 * n, 256)
        outp_ref[cols, :] = dot_tn(g[:, cols], att_ref[...]).astype(bf16)

    @pl.when(yh == 0)
    def _():
        give_kv.wait_recv()

        def body(r):
            gkv[r] += take[r].astype(f32)

        by_rows(HALF_KEYS, body, 64)

    def back_key(r):
        back_head(r, 2, gkv[r, 0:128])
        gp_ref[r, 384:512] = gkv[r, 128:256].astype(bf16)

    by_rows(HALF_KEYS, back_key, 64)
    planes.turn()
    planes.relay2()
    gather.drain()

    @pl.when(yh == 1)
    def _():
        give_kv.wait_send()

    planes.finish()
    swap.start()
    swap.finish()
    swap.drain()
    planes.drain()


def back(gbr, wa, wb, att, q, kv, okv, qseg, kseg, hid, mid, proj, tab, gains, part, cid):
    return pl.pallas_call(
        back_kernel,
        out_shape=(
            struct((ROWS, D), bf16),
            struct((HALF_KEYS, 512), bf16),
            struct((8, 128), f32),
            struct((D, 256), bf16),
            struct((GROUP, 16, B_WIDTH), bf16),
        ),
        in_specs=[VM, ANY, ANY] + [VM] * 11 + [ANY],
        out_specs=(VM, VM, VM, VM, ANY),
        scratch_shapes=[
            pltpu.VMEM((HALF_KEYS, D), bf16),
            pltpu.VMEM((D, 256), bf16),
            pltpu.VMEM((D, 768), bf16),
            pltpu.VMEM((HALF_KEYS, D), bf16),
            pltpu.VMEM((HALF_KEYS, 256), bf16),
            pltpu.VMEM((KEYS, 256), f32),
            pltpu.VMEM((KEYS, 256), f32),
            pltpu.VMEM((1, 256), f32),
            pltpu.VMEM((1, 256), f32),
            pltpu.VMEM((HALF_KEYS, 256), f32),
            pltpu.VMEM((HALF_KEYS, 256), f32),
            pltpu.VMEM((HALF_KEYS, 256), f32),
            pltpu.VMEM((HALF_KEYS, 256), bf16),
            pltpu.VMEM((HALF_KEYS, 256), bf16),
            DMA((2,)),
            DMA((2,)),
        ]
        + GATHER_SCRATCH
        + scatter_scratch()
        + plane_scatter_scratch(B_WIDTH)
        + SWAP_SCRATCH,
        compiler_params=params(cid, 60),
        name="back",
    )(gbr, wa, wb, att, q, kv, okv, qseg, kseg, hid, mid, proj, tab, gains, part.reshape(4, 4, ROWS, B_WIDTH))


def last_kernel(
    gp_ref, n_ref, wa_ref, outp_ref, gsum_ref, tok_ref, gmid_ref,
    tg_ref, owned_ref,
    n, wq, p, pa, sems, *rest,
):
    sib_in, s_acc, near, fwd, r_send, r_recv = rest[:6]
    buffers, (s_own, s_send, s_recv) = rest[6 : 6 + PLANE_SCATTER], rest[6 + PLANE_SCATTER :]
    z, c, up, dn, far = ring_place()
    x, y = plane_place()
    get_n = pltpu.make_async_copy(n_ref, n, sems.at[0])
    get_wq = pltpu.make_async_copy(wa_ref.at[:, pl.ds(0, 512)], wq, sems.at[1])
    get_out = pltpu.make_async_copy(outp_ref, pa.at[:, :, :, pl.ds(640, 256)], sems.at[2])
    get_n.start()
    get_out.start()
    get_wq.start()
    greet(group_targets(2 * z + c) + plane_targets(x, y))
    scatter = RowScatter(p, sib_in, s_acc, near, fwd, r_send, r_recv)
    planes = PlaneScatter(pa, buffers)
    swap = swap_last(planes.last, owned_ref, s_own, s_send, s_recv)

    gains = jnp.concatenate([gsum_ref[...], jnp.zeros((120, 128), f32)], axis=0).astype(bf16)
    col = lax.broadcasted_iota(jnp.int32, (ROWS, 128), 1)
    row = lax.broadcasted_iota(jnp.int32, (ROWS, 128), 0)
    for k in range(16):
        pick = (row + ROWS * k == 16 * col).astype(bf16)
        pa[k // 4, k % 4, :, 512:640] = dot_nt(pick, gains).astype(bf16)
    get_n.wait()
    for i in range(8):
        v = dot_tn(n[:, 256 * i : 256 * i + 256], gp_ref[...]).astype(bf16)
        for k in range(2):
            b = 2 * i + k
            pa[b // 4, b % 4, :, 0:512] = v[ROWS * k : ROWS * k + ROWS]
    get_out.wait()
    planes.start()
    get_wq.wait()
    for k, zz in enumerate(scatter.order):
        rows = span(256 * zz, 256, 256)
        for m in range(4):
            cols = pl.ds(512 * m, 512)
            p[rows, cols] = dot_nt(gp_ref[rows, :], wq[cols, :]).astype(bf16)
        scatter.swap(k)
        if k:
            scatter.add(k - 1)
    planes.relay()
    scatter.relay()
    planes.turn()

    def close(r, t):
        v = tok_ref[r].astype(f32)
        s = lax.rsqrt(jnp.mean(v * v, axis=-1, keepdims=True) + EPS)
        hat = v * s
        tg_ref[r] = gmid_ref[r] + s * (t - hat * jnp.mean(t * hat, axis=-1, keepdims=True))

    planes.relay2()
    scatter.finish(close)
    planes.finish()
    swap.start()
    swap.finish()
    swap.drain()
    planes.drain()


def last(gp, n_full, wa, outp, gsum, tokens, gmid, cid):
    return pl.pallas_call(
        last_kernel,
        out_shape=(struct((ROWS, D), f32), struct((GROUP, 16, A_WIDTH), bf16)),
        in_specs=[VM, ANY, ANY, ANY, VM, VM, VM],
        out_specs=(VM, ANY),
        scratch_shapes=[
            pltpu.VMEM((HALF_KEYS, D), bf16),
            pltpu.VMEM((D, 512), bf16),
            pltpu.VMEM((HALF_KEYS, D), bf16),
            pltpu.VMEM((4, 4, ROWS, A_WIDTH), bf16),
            DMA((3,)),
        ]
        + scatter_scratch()
        + plane_scatter_scratch(A_WIDTH)
        + SWAP_SCRATCH,
        compiler_params=params(cid, 60),
        name="last",
    )(gp, n_full, wa, outp.reshape(4, 4, ROWS, 256), gsum, tokens, gmid)


def unchunk(g, parts):
    pieces = []
    at = 0
    for width in parts:
        pieces.append(g[:, :, at : at + width].transpose(1, 0, 2).reshape(16, GROUP * width))
        at += width
    return jnp.concatenate(pieces, axis=1)


def local(
    tokens,
    cotangent,
    seq_rows,
    qkv_weight,
    out_weight,
    attn_gain,
    query_gain,
    key_gain,
    gate_up_weight,
    down_weight,
    mlp_gain,
):
    yh = lax.axis_index("yh")
    counts = seq_rows[0]
    position_all, segment = row_layout(counts, jnp.arange(16, dtype=jnp.int32)[:, None], ROWS)
    own_position = lax.dynamic_slice_in_dim(position_all.reshape(KEYS), yh * HALF_KEYS, HALF_KEYS)
    segment = jnp.tile(segment, 16)
    segment = jnp.where(segment < 0, 2 + jnp.arange(KEYS, dtype=jnp.int32), segment)
    own_segment = lax.dynamic_slice_in_dim(segment, yh * HALF_KEYS, HALF_KEYS)
    both_segments = jnp.stack([own_segment, segment[:HALF_KEYS]])

    n_full, wa, own_b, projected, q, kv, gains, tables = front(
        tokens,
        qkv_weight,
        out_weight,
        gate_up_weight,
        down_weight,
        attn_gain[:, None],
        mlp_gain[:, None],
        jnp.pad(jnp.concatenate([query_gain, key_gain]), (0, 126))[None],
        own_position.astype(f32)[:, None],
        0,
    )
    wb, c_full, other_kv, attended, middle, mhat = attend(
        q, kv, own_segment[:, None], both_segments, own_b, cotangent, wa, tokens, 1
    )
    hidden, g_middle, g_branch, mlp_part = mlp(mhat, middle, cotangent, c_full, wb, 2)
    block_out, g_projected, gain_sums, out_part, owned_b = back(
        g_branch,
        wa,
        wb,
        attended,
        q,
        kv,
        other_kv,
        own_segment[None],
        both_segments[:, :, None],
        hidden,
        middle,
        projected,
        tables,
        gains,
        mlp_part,
        3,
    )
    tokens_grad, owned = last(g_projected, n_full, wa, out_part, gain_sums, tokens, g_middle, 4)
    owned = owned.astype(f32)
    owned_b = owned_b.astype(f32)
    qkv_raw = unchunk(owned[:, :, :512], (256, 128, 128))
    gain_grads = jnp.sum(owned[:, 0, 512:514], axis=0)
    out_grad = unchunk(owned[:, :, 640:896], (256,))
    gate_up_raw = unchunk(owned_b[:, :, :1536], (768, 768))
    down_grad = unchunk(owned_b[:, :, 1536:], (768,))
    return (
        block_out,
        tokens_grad,
        qkv_raw * attn_gain.astype(f32)[:, None],
        out_grad,
        jnp.sum(qkv_raw * qkv_weight.astype(f32), axis=1),
        gain_grads[:1],
        gain_grads[1:],
        gate_up_raw * mlp_gain.astype(f32)[:, None],
        down_grad,
        jnp.sum(gate_up_raw * gate_up_weight.astype(f32), axis=1),
    )


def solution(mesh):
    fine = Mesh(mesh.devices.reshape(4, 2, 2, 4, 2), AXES)
    rows2 = P(AXES, None)
    rows1 = P(AXES)
    return jax.shard_map(
        local,
        mesh=fine,
        in_specs=(
            rows2,
            rows2,
            P(("x", "yl"), None),
            rows2,
            rows2,
            rows1,
            rows1,
            rows1,
            rows2,
            rows2,
            rows1,
        ),
        out_specs=(
            rows2,
            rows2,
            rows2,
            rows2,
            rows1,
            rows1,
            rows1,
            rows2,
            rows2,
            rows1,
        ),
        check_vma=False,
    )
```

```python
import math

import jax
import jax.numpy as jnp
from jax import lax
from jax.experimental import pallas as pl
from jax.experimental.pallas import tpu as pltpu
from jax.sharding import Mesh
from jax.sharding import PartitionSpec as P

HEAD_SIZE = 128
FF = 6144
ROWS = 128
GROUP = 8
HALF_KEYS = ROWS * GROUP
KEYS = 2 * HALF_KEYS
SCALE = HEAD_SIZE**-0.5
WIDTH = 3200
EPS = 1e-6
ROPE_BASE = 1000000.0
AXES = ("x", "yl", "yh", "z", "c")
TP = ("z", "c")
PLANE = ("x", "yl", "yh")
f32 = jnp.float32
bf16 = jnp.bfloat16


def dot(a, b):
    return jnp.dot(a, b, preferred_element_type=f32)


def dot_nt(a, b):
    return lax.dot_general(a, b, (((1,), (1,)), ((), ())), preferred_element_type=f32)


def dot_tn(a, b):
    return lax.dot_general(a, b, (((0,), (0,)), ((), ())), preferred_element_type=f32)


MESH = pl.DeviceIdType.MESH
ANY = pl.BlockSpec(memory_space=pl.ANY)
VM = pl.BlockSpec(memory_space=pltpu.VMEM)
SM = pl.BlockSpec(memory_space=pltpu.SMEM)
DMA = pltpu.SemaphoreType.DMA
HALF = 64
D = 2048
A_WIDTH = 896
B_WIDTH = 2304
LOG2E = 1.4426950408889634
scope = jax.named_scope


def params(cid=None, mib=56):
    if cid is None:
        return pltpu.CompilerParams(vmem_limit_bytes=mib << 20)
    return pltpu.CompilerParams(
        collective_id=cid, has_side_effects=True, vmem_limit_bytes=mib << 20
    )


def struct(shape, dtype):
    return jax.ShapeDtypeStruct(shape, dtype)


def rcopy(src, dst, send, recv, to):
    return pltpu.make_async_remote_copy(
        src, dst, send, recv, device_id=to, device_id_type=MESH
    )


def span(start, size, step=16):
    return pl.ds(pl.multiple_of(start, step), size)


def by_rows(rows, body, step=16):
    def run(i, carry):
        body(span(i * step, step, step))
        return carry

    lax.fori_loop(0, rows // step, run, 0)


def ring_place():
    z, c = lax.axis_index("z"), lax.axis_index("c")
    return z, c, lax.rem(z + 1, 4), lax.rem(z + 3, 4), lax.rem(z + 2, 4)


def plane_place():
    return lax.axis_index("x"), lax.axis_index("yh") * 2 + lax.axis_index("yl")


def y_slot(y):
    return lax.rem(y, 2) * 2 + y // 2


def slot(x, y):
    return x * 4 + y_slot(y)


def to_x(x):
    return {"x": x}


def to_y(y):
    return {"yl": lax.rem(y, 2), "yh": y // 2}


def to_group(j):
    return {"z": j // 2, "c": lax.rem(j, 2)}


def hail(targets):
    barrier = pltpu.get_barrier_semaphore()
    for to in targets:
        pl.semaphore_signal(barrier, inc=1, device_id=to, device_id_type=MESH)
    return len(targets)


def await_all(count):
    pl.semaphore_wait(pltpu.get_barrier_semaphore(), count)


def ring_targets():
    z, c, up, dn, far = ring_place()
    return [{"z": up}, {"z": dn}, {"c": 1 - c}]


def group_targets(me):
    return [to_group(lax.rem(me + d, GROUP)) for d in range(1, GROUP)]


def plane_targets(x, y):
    return [to_x(lax.rem(x + s, 4)) for s in (1, 2, 3)] + [
        to_y(lax.rem(y + s, 4)) for s in (1, 2, 3)
    ]


class RowGather:
    def __init__(self, src, dst, own_sem, send, recv):
        z, c, up, dn, far = ring_place()
        low, high = pl.ds(0, HALF), pl.ds(HALF, HALF)

        def at(zz, part=None):
            first = (2 * zz + c) * ROWS
            if part is None:
                return dst.at[span(first, ROWS)]
            return dst.at[span(first + part * HALF, HALF)]

        to_up, to_dn, to_sib = {"z": up}, {"z": dn}, {"c": 1 - c}
        plan = [
            (src.at[low], at(z, 0), to_up),
            (src.at[high], at(z, 1), to_up),
            (at(dn, 0), at(dn, 0), to_up),
            (src.at[high], at(z, 1), to_dn),
            (src.at[low], at(z, 0), to_dn),
            (at(up, 1), at(up, 1), to_dn),
            (src, at(z), to_sib),
            (at(dn), at(dn), to_sib),
            (at(up), at(up), to_sib),
            (at(far, 0), at(far, 0), to_sib),
            (at(far, 1), at(far, 1), to_sib),
        ]
        self.cp = [rcopy(a, b, send.at[i], recv.at[i], to) for i, (a, b, to) in enumerate(plan)]
        self.own = pltpu.make_async_copy(src, at(z), own_sem)

    def start(self):
        self.own.start()
        for i in (0, 3, 1, 4, 6):
            self.cp[i].start()

    def relay(self):
        cp = self.cp
        cp[0].wait_recv()
        cp[2].start()
        cp[3].wait_recv()
        cp[5].start()

    def share(self):
        cp = self.cp
        cp[1].wait_recv()
        cp[7].start()
        cp[4].wait_recv()
        cp[8].start()

    def have_own(self):
        self.own.wait()
        self.cp[6].wait_recv()

    def have_dn(self):
        self.cp[7].wait_recv()

    def have_up(self):
        self.cp[8].wait_recv()

    def share_far(self):
        cp = self.cp
        cp[2].wait_recv()
        cp[9].start()
        cp[5].wait_recv()
        cp[10].start()

    def have_far(self):
        self.cp[9].wait_recv()
        self.cp[10].wait_recv()

    def drain(self):
        for c in self.cp:
            c.wait_send()


GATHER_SCRATCH = [DMA((1,)), DMA((11,)), DMA((11,))]


def scatter_scratch(n=D):
    return [
        pltpu.VMEM((4, ROWS, n), bf16),
        pltpu.VMEM((3, ROWS, n), bf16),
        pltpu.VMEM((2, ROWS, n), bf16),
        pltpu.VMEM((2, HALF, n), bf16),
        DMA((10,)),
        DMA((10,)),
    ]


class RowScatter:
    def __init__(self, p, sib_in, acc, near, fwd, send, recv):
        z, c, up, dn, far = ring_place()
        self.order = (far, up, dn, z)
        self.p, self.sib_in, self.acc, self.near, self.fwd, self.c = p, sib_in, acc, near, fwd, c
        low, high = pl.ds(0, HALF), pl.ds(HALF, HALF)
        to_up, to_dn, to_sib = {"z": up}, {"z": dn}, {"c": 1 - c}
        self.sib = [
            rcopy(
                p.at[span((2 * zz + 1 - c) * ROWS, ROWS)],
                sib_in.at[k],
                send.at[k],
                recv.at[k],
                to_sib,
            )
            for k, zz in enumerate(self.order)
        ]
        plan = [
            (acc.at[0, low], fwd.at[0], to_dn),
            (acc.at[0, high], fwd.at[1], to_up),
            (acc.at[1, low], near.at[1, low], to_up),
            (acc.at[1, high], near.at[1, high], to_up),
            (acc.at[2, high], near.at[0, high], to_dn),
            (acc.at[2, low], near.at[0, low], to_dn),
        ]
        self.cp = [
            rcopy(a, b, send.at[4 + i], recv.at[4 + i], to) for i, (a, b, to) in enumerate(plan)
        ]

    def swap(self, k):
        self.sib[k].start()

    def add(self, k):
        self.sib[k].wait_recv()
        first = (2 * self.order[k] + self.c) * ROWS

        def body(r):
            mine = self.p[span(first + r.start, 16)].astype(f32)
            self.acc[k, r] = (mine + self.sib_in[k, r].astype(f32)).astype(bf16)

        by_rows(ROWS, body)
        if k == 0:
            self.cp[0].start()
            self.cp[1].start()
        else:
            self.cp[2 * k].start()

    def relay(self):
        for arrive, k, part, then in ((1, 1, 1, 3), (0, 2, 0, 5)):
            self.cp[arrive].wait_recv()

            def body(r):
                at = span(part * HALF + r.start, 16)
                t = self.acc[k, at].astype(f32) + self.fwd[part, r].astype(f32)
                self.acc[k, at] = t.astype(bf16)

            by_rows(HALF, body)
            self.cp[then].start()

    def finish(self, body):
        self.sib[3].wait_recv()
        for i in (2, 3, 4, 5):
            self.cp[i].wait_recv()
        first = (2 * self.order[3] + self.c) * ROWS

        def run(r):
            t = self.p[span(first + r.start, 16)].astype(f32) + self.sib_in[3, r].astype(f32)
            t += self.near[0, r].astype(f32) + self.near[1, r].astype(f32)
            body(r, t)

        by_rows(ROWS, run)
        for s in self.sib + self.cp:
            s.wait_send()


class Ring:
    def __init__(self, axis, at, block, first, rows, send, recv):
        step = to_x if axis == "x" else to_y
        up, dn = lax.rem(at + 1, 4), lax.rem(at + 3, 4)

        def part(who, start, size):
            return block[0].at[span(block[1](who) * ROWS + start, size)]

        half = rows // 2
        plan = [
            (part(at, first, rows), step(up)),
            (part(at, first, rows), step(dn)),
            (part(dn, first, half), step(up)),
            (part(up, first + half, half), step(dn)),
        ]
        self.cp = [rcopy(r, r, send.at[i], recv.at[i], to) for i, (r, to) in enumerate(plan)]

    def start(self):
        self.cp[0].start()
        self.cp[1].start()

    def relay(self):
        self.cp[0].wait_recv()
        self.cp[2].start()
        self.cp[1].wait_recv()
        self.cp[3].start()

    def finish(self):
        self.cp[2].wait_recv()
        self.cp[3].wait_recv()

    def drain(self):
        for c in self.cp:
            c.wait_send()


class PlaneGather:
    def __init__(self, dst, send, recv):
        x, y = plane_place()
        self.halves = []
        for half in (0, 1):

            def ring(axis, other, k):
                if axis == "x":
                    block, at = (dst, lambda who: slot(who, other)), x
                else:
                    block, at = (dst, lambda who: slot(other, who)), y
                return Ring(axis, at, block, half * HALF, HALF, send.at[half, k], recv.at[half, k])

            axes = ("y", "x") if half == 0 else ("x", "y")
            here, over = (y, x) if half == 0 else (x, y)
            others = [here, lax.rem(here + 3, 4), lax.rem(here + 1, 4), lax.rem(here + 2, 4)]
            self.halves.append(
                [ring(axes[0], over, 0)] + [ring(axes[1], o, 1 + k) for k, o in enumerate(others)]
            )

    def both(self, k, what):
        for half in self.halves:
            getattr(half[k], what)()

    def one(self):
        self.both(0, "start")
        self.both(1, "start")

    def two(self):
        self.both(0, "relay")
        self.both(2, "start")
        self.both(3, "start")

    def three(self):
        self.both(1, "relay")
        self.both(0, "finish")
        self.both(4, "start")

    def four(self):
        self.both(2, "relay")
        self.both(3, "relay")

    def five(self):
        self.both(4, "relay")

    def finish(self):
        for k in range(1, 5):
            self.both(k, "finish")
        for k in range(5):
            self.both(k, "drain")


PLANE_SCRATCH = [DMA((2, 5, 4)), DMA((2, 5, 4))]


class GroupSwap:
    def __init__(self, src, dst, own_sem, send, recv):
        z, c, up, dn, far = ring_place()
        me = 2 * z + c
        self.own = pltpu.make_async_copy(src(me), dst(me), own_sem)
        self.cp = []
        for d in range(1, GROUP):
            j = lax.rem(me + d, GROUP)
            self.cp.append(rcopy(src(j), dst(me), send.at[d - 1], recv.at[d - 1], to_group(j)))

    def start(self):
        self.own.start()
        for s in self.cp:
            s.start()

    def finish(self):
        self.own.wait()
        for s in self.cp:
            s.wait_recv()

    def drain(self):
        for s in self.cp:
            s.wait_send()


SWAP_SCRATCH = [DMA((1,)), DMA((7,)), DMA((7,))]


def segment_of(index, counts):
    place = lax.rem(index, ROWS)
    first, both = counts[0, 0], counts[0, 0] + counts[0, 1]
    return jnp.where(place < first, 0, jnp.where(place < both, 1, 2 + index))


def position_of(index, counts):
    place, device = lax.rem(index, ROWS), index // ROWS
    first, second = counts[0, 0], counts[0, 1]
    inner = jnp.where(place < first + second, device * second + place - first, place)
    return jnp.where(place < first, device * first + place, inner)


def column(start, size):
    return start + lax.broadcasted_iota(jnp.int32, (size, 1), 0)


def line(start, size):
    return start + lax.broadcasted_iota(jnp.int32, (1, size), 1)


def upright(values):
    row = lax.broadcasted_iota(jnp.int32, (16, 16), 0)
    col = lax.broadcasted_iota(jnp.int32, (16, 16), 1)
    return jnp.sum(jnp.where(row == col, values, 0.0), axis=1, keepdims=True)


def turn(values):
    return pltpu.roll(values, 64, 1)


def weigh(q, keys, values, ok):
    p = jnp.where(ok, jnp.exp2(dot_nt(q, keys) * (SCALE * LOG2E)), 0.0)
    return jnp.sum(p, axis=1, keepdims=True), dot(p.astype(bf16), values)


def forward_kernel(
    tok_ref, qkv_ref, out_ref, gu_ref, dw_ref, ga_ref, gm_ref, qg_ref, kg_ref, cot_ref, counts,
    n_out, wa_out, wb, c_out, m_out, proj_ref, q_ref, kv_ref, okv_ref, att_ref, gains_ref, tab_ref, mid_ref,
    xh, pa, pb, n, wa, acc, tot, p, store_sems, kv_sems, *rest,
):
    x_own, x_send, x_recv, c_own, c_send, c_recv, m_own, m_send, m_recv = rest[:9]
    sa_own, sa_send, sa_recv, sb_own, sb_send, sb_recv = rest[9:15]
    wa_send, wa_recv, wb_send, wb_recv = rest[15:19]
    yh = lax.axis_index("yh")
    here = HALF_KEYS * yh
    z, c, up, dn, far = ring_place()
    me = 2 * z + c
    x, y = plane_place()
    greeted = hail(group_targets(me) + plane_targets(x, y))

    def norm(r):
        t = tok_ref[r].astype(f32)
        xh[r] = (t * lax.rsqrt(jnp.mean(t * t, axis=-1, keepdims=True) + EPS)).astype(bf16)

    by_rows(ROWS, norm)
    ga, gm = upright(ga_ref[...].astype(f32)), upright(gm_ref[...].astype(f32))
    lane = lax.broadcasted_iota(jnp.int32, (16, 128), 1)
    query_gain = jnp.broadcast_to(qg_ref[...].astype(f32), (16, 128))
    key_gain = jnp.broadcast_to(kg_ref[...].astype(f32), (16, 128))
    head_gains = jnp.where(lane == 0, query_gain, jnp.where(lane == 1, key_gain, 0.0)).astype(bf16)
    for j in range(GROUP):
        pa[j, :, 0:256] = (qkv_ref[:, 256 * j : 256 * j + 256].astype(f32) * ga).astype(bf16)
        for k in range(2):
            first = 2048 + 1024 * k + 128 * j
            pa[j, :, 256 + 128 * k : 384 + 128 * k] = (
                qkv_ref[:, first : first + 128].astype(f32) * ga
            ).astype(bf16)
        pa[j, :, 512:640] = head_gains
        pa[j, :, 640:896] = out_ref[:, 256 * j : 256 * j + 256]
        for k in range(2):
            first = 6144 * k + 768 * j
            pb[j, :, 768 * k : 768 * k + 768] = (
                gu_ref[:, first : first + 768].astype(f32) * gm
            ).astype(bf16)
        pb[j, :, 1536:2304] = dw_ref[:, 768 * j : 768 * j + 768]

    await_all(greeted)
    own_slot = slot(x, y) * ROWS
    swap_a = GroupSwap(
        lambda j: pa.at[j], lambda j: wa.at[span(own_slot + 16 * j, 16)], sa_own.at[0], sa_send, sa_recv
    )
    swap_b = GroupSwap(
        lambda j: pb.at[j], lambda j: wb.at[span(own_slot + 16 * j, 16)], sb_own.at[0], sb_send, sb_recv
    )
    gather_x = RowGather(xh, n, x_own.at[0], x_send, x_recv)
    gather_c = RowGather(cot_ref, c_out, c_own.at[0], c_send, c_recv)
    gather_m = RowGather(xh, m_out, m_own.at[0], m_send, m_recv)
    plane_a = PlaneGather(wa, wa_send, wa_recv)
    plane_b = PlaneGather(wb, wb_send, wb_recv)
    scatter = RowScatter(p, *rest[19:])
    blocks = (z, dn, up, far)
    gives = [
        rcopy(
            kv_ref.at[span(256 * zz, 256, 256)],
            okv_ref.at[span(256 * zz, 256, 256)],
            kv_sems.at[0, k],
            kv_sems.at[1, k],
            {"yh": 1 - yh},
        )
        for k, zz in enumerate(blocks)
    ]
    swap_a.start()
    gather_x.start()

    lane = lax.broadcasted_iota(jnp.int32, (1, 128), 1)
    k = lax.rem(lane, 64).astype(f32)
    freq = jnp.exp(k * (-2.0 * math.log(ROPE_BASE) / HEAD_SIZE))
    sign = jnp.where(lane < 64, -1.0, 1.0)

    def table(r):
        index = column(r.start + here, 64)
        angle = position_of(index, counts).astype(f32) * freq
        tab_ref[0, r] = jnp.cos(angle)
        tab_ref[1, r] = jnp.sin(angle) * sign

    swap_a.finish()
    plane_a.one()
    by_rows(HALF_KEYS, table, 64)
    plane_a.two()
    gather_x.relay()
    plane_a.three()
    gather_x.share()
    plane_a.four()
    plane_a.five()
    gather_x.share_far()
    swap_b.start()
    plane_a.finish()
    store_w = pltpu.make_async_copy(wa, wa_out, store_sems.at[1])
    store_w.start()

    row = lax.broadcasted_iota(jnp.int32, (D, 128), 0)
    col = lax.broadcasted_iota(jnp.int32, (D, 128), 1)
    pick = (row == 16 * col).astype(bf16)
    gains = dot_tn(wa[:, 512:640], pick)[0:8]
    gains_ref[...] = gains

    def project(zz):
        rows = span(256 * zz, 256, 256)
        proj_ref[rows, :] = dot(n[rows, :], wa[:, 0:512])

        def shape(r):
            r = span(256 * zz + r.start, 64, 64)
            for h in range(3):
                v = proj_ref[r, 128 * h : 128 * h + 128]
                g = gains[0:1] if h < 2 else gains[1:2]
                u = v * lax.rsqrt(jnp.mean(v * v, axis=-1, keepdims=True) + EPS) * g
                o = (u * tab_ref[0, r] + turn(u) * tab_ref[1, r]).astype(bf16)
                if h < 2:
                    q_ref[r, 128 * h : 128 * h + 128] = o
                else:
                    kv_ref[r, 0:128] = o
            kv_ref[r, 128:256] = proj_ref[r, 384:512].astype(bf16)

        by_rows(256, shape, 64)

    def block(k):
        project(blocks[k])

        @pl.when(yh == 0)
        def _():
            gives[k].start()

    gather_x.have_own()
    block(0)
    gather_x.have_dn()
    block(1)
    gather_x.have_up()
    block(2)
    gather_x.have_far()
    block(3)
    swap_b.finish()
    plane_b.one()
    gather_c.start()

    @pl.when(yh == 0)
    def _():
        okv_ref[...] = jnp.zeros_like(okv_ref)

    store_n = pltpu.make_async_copy(n, n_out, store_sems.at[0])
    store_n.start()

    def near_keys(h):
        cols = pl.ds(128 * h, 128)
        for i in range(4):
            rows = pl.ds(256 * i, 256)
            q = q_ref[rows, cols]
            t = jnp.zeros((256, 1), f32)
            a = jnp.zeros((256, 128), f32)
            for k in range(i + 1):
                keys = pl.ds(256 * k, 256)
                ok = segment_of(column(256 * i + here, 256), counts) == segment_of(
                    line(256 * k + here, 256), counts
                )
                if k == i:
                    ok &= lax.broadcasted_iota(jnp.int32, (256, 256), 0) >= lax.broadcasted_iota(
                        jnp.int32, (256, 256), 1
                    )
                dt, da = weigh(q, kv_ref[keys, 0:128], kv_ref[keys, 128:256], ok)
                t += dt
                a += da
            acc[rows, cols] = a
            tot[h, rows] = t

    def far_keys(zz):
        rows = span(256 * zz, 256, 256)
        for h in range(2):
            cols = pl.ds(128 * h, 128)
            q = q_ref[rows, cols]
            t = tot[h, rows]
            a = acc[rows, cols]
            for k in range(4):
                keys = pl.ds(256 * k, 256)
                ok = segment_of(column(256 * zz + here, 256), counts) == segment_of(
                    line(256 * k, 256), counts
                )
                dt, da = weigh(q, okv_ref[keys, 0:128], okv_ref[keys, 128:256], ok)
                t += dt
                a += da
            tot[h, rows] = t
            acc[rows, cols] = a

    near_keys(0)
    near_keys(1)
    gather_c.relay()
    plane_b.two()

    @pl.when(yh == 1)
    def _():
        for g in gives:
            g.wait_recv()

    for k, zz in enumerate(scatter.order):
        rows = span(256 * zz, 256, 256)

        @pl.when(yh == 1)
        def _():
            far_keys(zz)

        for h in range(2):
            cols = pl.ds(128 * h, 128)
            att_ref[rows, cols] = (acc[rows, cols] / tot[h, rows]).astype(bf16)
        for b in range(4):
            cols = pl.ds(512 * b, 512)
            p[rows, cols] = dot_nt(att_ref[rows, :], wa[cols, 640:896]).astype(bf16)
        scatter.swap(k)
        if k:
            scatter.add(k - 1)
        if k == 1:
            gather_c.share()

    @pl.when(yh == 0)
    def _():
        for g in gives:
            g.wait_send()

    plane_b.three()
    gather_c.share_far()
    scatter.relay()
    plane_b.four()

    def close(r, t):
        m = tok_ref[r].astype(f32) + t
        mid_ref[r] = m
        xh[r] = (m * lax.rsqrt(jnp.mean(m * m, axis=-1, keepdims=True) + EPS)).astype(bf16)

    gather_x.drain()
    scatter.finish(close)
    gather_m.start()
    gather_c.have_own()
    gather_c.have_dn()
    gather_c.have_up()
    gather_c.have_far()
    plane_b.five()
    gather_m.relay()
    gather_m.share()
    gather_m.share_far()
    plane_b.finish()
    gather_m.have_own()
    gather_m.have_dn()
    gather_m.have_up()
    gather_m.have_far()
    gather_c.drain()
    gather_m.drain()
    swap_a.drain()
    swap_b.drain()
    store_n.wait()
    store_w.wait()


def forward(tokens, qkv, out, gu, dw, ga, gm, qg, kg, cot, counts, cid):
    return pl.pallas_call(
        forward_kernel,
        out_shape=(
            struct((HALF_KEYS, D), bf16),
            struct((D, A_WIDTH), bf16),
            struct((D, B_WIDTH), bf16),
            struct((HALF_KEYS, D), bf16),
            struct((HALF_KEYS, D), bf16),
            struct((HALF_KEYS, 512), f32),
            struct((HALF_KEYS, 256), bf16),
            struct((HALF_KEYS, 256), bf16),
            struct((HALF_KEYS, 256), bf16),
            struct((HALF_KEYS, 256), bf16),
            struct((8, 128), f32),
            struct((2, HALF_KEYS, 128), f32),
            struct((ROWS, D), f32),
        ),
        in_specs=[VM] * 10 + [SM],
        out_specs=(ANY,) * 5 + (VM,) * 8,
        scratch_shapes=[
            pltpu.VMEM((ROWS, D), bf16),
            pltpu.VMEM((GROUP, 16, A_WIDTH), bf16),
            pltpu.VMEM((GROUP, 16, B_WIDTH), bf16),
            pltpu.VMEM((HALF_KEYS, D), bf16),
            pltpu.VMEM((D, A_WIDTH), bf16),
            pltpu.VMEM((HALF_KEYS, 256), f32),
            pltpu.VMEM((2, HALF_KEYS, 1), f32),
            pltpu.VMEM((HALF_KEYS, D), bf16),
            DMA((2,)),
            DMA((2, 4)),
        ]
        + GATHER_SCRATCH * 3
        + SWAP_SCRATCH * 2
        + PLANE_SCRATCH * 2
        + scatter_scratch(),
        compiler_params=params(cid),
        name="forward",
    )(tokens, qkv, out, gu, dw, ga, gm, qg, kg, cot, counts)


def mlp_kernel(
    m_ref, mid_ref, cot_ref, c_ref, wb_ref,
    po_ref, gmid_ref, gbr_ref, grad_ref,
    m, cb, wb, hid, gj, p, p2, stage, sems, stage_sems, out_sems, *rest,
):
    z, c, up, dn, far = ring_place()
    get_w = pltpu.make_async_copy(wb_ref, wb, sems.at[0])
    get_m = pltpu.make_async_copy(m_ref, m, sems.at[1])
    get_c = pltpu.make_async_copy(c_ref, cb, sems.at[2])
    get_w.start()
    get_m.start()
    get_c.start()
    await_all(hail(ring_targets()))
    scatter = RowScatter(p, *rest)
    get_w.wait()
    get_m.wait()
    get_c.wait()

    def block(zz):
        rows = span(256 * zz, 256, 256)
        for t in range(3):
            gate_cols, up_cols = pl.ds(256 * t, 256), pl.ds(768 + 256 * t, 256)
            gate = dot(m[rows, :], wb[:, gate_cols])
            upper = dot(m[rows, :], wb[:, up_cols])
            gh = dot(cb[rows, :], wb[:, 1536 + 256 * t : 1792 + 256 * t])
            sig = 1.0 / (1.0 + jnp.exp(-gate))
            act = gate * sig
            hid[rows, gate_cols] = (act * upper).astype(bf16)
            gj[rows, up_cols] = (gh * act).astype(bf16)
            gj[rows, gate_cols] = (gh * upper * (sig + act * (1.0 - sig))).astype(bf16)
        for n in range(4):
            cols = pl.ds(512 * n, 512)
            p[rows, cols] = dot_nt(gj[rows, :], wb[cols, 0:1536]).astype(bf16)

    for k, zz in enumerate(scatter.order):
        block(zz)
        scatter.swap(k)
        if k:
            scatter.add(k - 1)

    def put(i):
        return pltpu.make_async_copy(
            stage.at[lax.rem(i, 2)], grad_ref.at[span(256 * i, 256, 256)], stage_sems.at[lax.rem(i, 2)]
        )

    def grads(i, carry):
        @pl.when(i >= 2)
        def _():
            put(i - 2).wait()

        cols = span(256 * i, 256, 256)
        s = lax.rem(i, 2)
        for n in range(3):
            part = pl.ds(512 * n, 512)
            stage[s, :, part] = dot_tn(m[:, cols], gj[:, part]).astype(bf16)
        stage[s, :, 1536:2304] = dot_tn(cb[:, cols], hid[...]).astype(bf16)
        put(i).start()
        return carry

    def close(r, t):
        v = mid_ref[r]
        s = lax.rsqrt(jnp.mean(v * v, axis=-1, keepdims=True) + EPS)
        hat = v * s
        g = cot_ref[r].astype(f32) + s * (t - hat * jnp.mean(t * hat, axis=-1, keepdims=True))
        gmid_ref[r] = g
        gbr_ref[r] = g.astype(bf16)

    scatter.relay()
    lax.fori_loop(0, 4, grads, 0)
    outs = []
    for i in range(4):
        rows = pl.ds(256 * i, 256)
        for n in range(4):
            cols = pl.ds(512 * n, 512)
            p2[rows, cols] = dot_nt(hid[rows, :], wb[cols, 1536:2304]).astype(bf16)
        outs.append(pltpu.make_async_copy(p2.at[rows], po_ref.at[rows], out_sems.at[i]))
        outs[i].start()
    lax.fori_loop(4, 8, grads, 0)
    scatter.finish(close)
    put(6).wait()
    put(7).wait()
    for o in outs:
        o.wait()


def mlp(m_full, middle, cot, c_full, wb, cid):
    return pl.pallas_call(
        mlp_kernel,
        out_shape=(
            struct((HALF_KEYS, D), bf16),
            struct((ROWS, D), f32),
            struct((ROWS, D), bf16),
            struct((D, B_WIDTH), bf16),
        ),
        in_specs=[ANY, VM, VM, ANY, ANY],
        out_specs=(ANY, VM, VM, ANY),
        scratch_shapes=[
            pltpu.VMEM((HALF_KEYS, D), bf16),
            pltpu.VMEM((HALF_KEYS, D), bf16),
            pltpu.VMEM((D, B_WIDTH), bf16),
            pltpu.VMEM((HALF_KEYS, 768), bf16),
            pltpu.VMEM((HALF_KEYS, 1536), bf16),
            pltpu.VMEM((HALF_KEYS, D), bf16),
            pltpu.VMEM((HALF_KEYS, D), bf16),
            pltpu.VMEM((2, 256, B_WIDTH), bf16),
            DMA((3,)),
            DMA((2,)),
            DMA((4,)),
        ]
        + scatter_scratch(),
        compiler_params=params(cid, 60),
        name="mlp",
    )(m_full, middle, cot, c_full, wb)


class RingSum:
    def __init__(self, step, at, src, own, fwd, near, rel, send, recv, load, lead):
        up, dn, far = lax.rem(at + 1, 4), lax.rem(at + 3, 4), lax.rem(at + 2, 4)
        n = 4 if lead else HALF
        lo, hi = pl.ds(0, n // 2), pl.ds(n // 2, n // 2)
        self.lead, self.half = lead, n // 2
        self.own, self.fwd, self.near, self.rel = own, fwd, near, rel
        plan = [
            (src(far).at[lo], fwd.at[0], step(dn)),
            (src(far).at[hi], fwd.at[1], step(up)),
            (src(up).at[lo], near.at[1, lo], step(up)),
            (rel.at[1], near.at[1, hi], step(up)),
            (src(dn).at[hi], near.at[0, hi], step(dn)),
            (rel.at[0], near.at[0, lo], step(dn)),
        ]
        self.cp = [rcopy(a, b, send.at[i], recv.at[i], to) for i, (a, b, to) in enumerate(plan)]
        self.loads = [
            pltpu.make_async_copy(a, b, load.at[i])
            for i, (a, b) in enumerate(
                [(src(at), own), (src(dn).at[lo], rel.at[0]), (src(up).at[hi], rel.at[1])]
            )
        ]

    def start(self):
        for i in (0, 1, 2, 4):
            self.cp[i].start()
        for c in self.loads:
            c.start()

    def tiles(self, whole, body):
        if self.lead:
            count = 16 if whole else 8

            def run(i, carry):
                body((i // 4, span(lax.rem(i, 4) * 16, 16)))
                return carry
        else:
            count = 4 if whole else 2

            def run(i, carry):
                body((span(i * 16, 16),))
                return carry

        lax.fori_loop(0, count, run, 0)

    def relay(self):
        for k, arrive, then in ((1, 1, 3), (0, 0, 5)):
            self.cp[arrive].wait_recv()
            self.loads[1 + k].wait()

            def body(at):
                t = self.rel[(k, *at)].astype(f32) + self.fwd[(k, *at)].astype(f32)
                self.rel[(k, *at)] = t.astype(bf16)

            self.tiles(False, body)
            self.cp[then].start()

    def finish(self):
        self.loads[0].wait()
        for i in (2, 3, 4, 5):
            self.cp[i].wait_recv()

        def body(at):
            t = self.own[at].astype(f32) + self.near[(0, *at)].astype(f32)
            self.own[at] = (t + self.near[(1, *at)].astype(f32)).astype(bf16)

        self.tiles(True, body)

    def drain(self):
        for c in self.cp:
            c.wait_send()


def plane_scatter_scratch(w):
    first = [pltpu.VMEM((4, HALF, w), bf16), pltpu.VMEM((2, 2, HALF, w), bf16), pltpu.VMEM((2, 4, HALF, w), bf16), pltpu.VMEM((2, 2, HALF, w), bf16)]
    second = [pltpu.VMEM((2, HALF // 2, w), bf16), pltpu.VMEM((2, HALF, w), bf16), pltpu.VMEM((2, HALF // 2, w), bf16)]
    return first * 2 + second * 2 + [pltpu.VMEM((ROWS, w), bf16), DMA((4, 6)), DMA((4, 6)), DMA((4, 3))]


PLANE_SCATTER = 18


class PlaneScatter:
    def __init__(self, src, buffers):
        x, y = plane_place()
        a1, b1, a2, b2 = buffers[0:4], buffers[4:8], buffers[8:11], buffers[11:14]
        self.last, send, recv, load = buffers[14:18]
        low, high = pl.ds(0, HALF), pl.ds(HALF, HALF)

        def ring(i, step, at, block, own, rest):
            return RingSum(step, at, block, own, *rest, send.at[i], recv.at[i], load.at[i], i < 2)

        own_a, own_b = a1[0], b1[0]
        self.first = [
            ring(0, to_x, x, lambda k: src.at[k, :, low], own_a, a1[1:]),
            ring(1, to_y, y, lambda k: src.at[:, y_slot(k), high], own_b, b1[1:]),
        ]
        self.second = [
            ring(2, to_y, y, lambda k: own_a.at[y_slot(k)], self.last.at[low], a2),
            ring(3, to_x, x, lambda k: own_b.at[k], self.last.at[high], b2),
        ]

    def start(self):
        for r in self.first:
            r.start()

    def relay(self):
        for r in self.first:
            r.relay()

    def turn(self):
        for r, s in zip(self.first, self.second):
            r.finish()
            s.start()

    def relay2(self):
        for r in self.second:
            r.relay()

    def finish(self):
        for r in self.second:
            r.finish()

    def drain(self):
        for r in self.first + self.second:
            r.drain()


def swap_last(last, out, own, send, recv):
    return GroupSwap(lambda j: last.at[span(16 * j, 16)], lambda j: out.at[j], own.at[0], send, recv)


def backward_kernel(
    gbr_ref, wa_ref, att_ref, q_ref, kv_ref, okv_ref, counts, proj_ref, tab_ref, gains_ref, part_ref, n_ref,
    tok_ref, gmid_ref, po_ref, mid_ref,
    tg_ref, bo_ref, owned_a_ref, owned_b_ref,
    g, wa, p, gatt, ps, gps, tot, inn, tots, inns, gq, gkv, gokv, give, take, gp, gsum, pa, sems, kv_sems, *rest,
):
    g_own, g_send, g_recv = rest[:3]
    sa_own, sa_send, sa_recv, sb_own, sb_send, sb_recv = rest[3:9]
    sib_in, s_acc, near, fwd, r_send, r_recv = rest[9:15]
    sib_in2, near2, fwd2, r_send2, r_recv2 = rest[15:20]
    rest = rest[20:]
    z, c, up, dn, far = ring_place()
    x, y = plane_place()
    yh = lax.axis_index("yh")
    here = HALF_KEYS * yh
    greeted = hail(group_targets(2 * z + c) + plane_targets(x, y))
    get_wa = pltpu.make_async_copy(wa_ref, wa, sems.at[0])
    get_wa.start()
    get_p = pltpu.make_async_copy(po_ref, p, sems.at[1])
    get_p.start()
    gather = RowGather(gbr_ref, g, g_own.at[0], g_send, g_recv)
    scatter = RowScatter(p, sib_in, s_acc, near, fwd, r_send, r_recv)
    scatter_o = RowScatter(p, sib_in2, s_acc, near2, fwd2, r_send2, r_recv2)
    planes_b = PlaneScatter(part_ref, rest[:PLANE_SCATTER])
    planes_a = PlaneScatter(pa, rest[PLANE_SCATTER:])
    swap_a = swap_last(planes_a.last, owned_a_ref, sa_own, sa_send, sa_recv)
    swap_b = swap_last(planes_b.last, owned_b_ref, sb_own, sb_send, sb_recv)
    give_kv = rcopy(give, take, kv_sems.at[0], kv_sems.at[1], {"yh": 1 - yh})
    await_all(greeted)
    gather.start()
    planes_b.start()
    gkv[...] = jnp.zeros_like(gkv)
    gokv[...] = jnp.zeros_like(gokv)
    gq[...] = jnp.zeros_like(gq)
    gsum[...] = jnp.zeros_like(gsum)
    get_wa.wait()
    get_p.wait()
    for k in range(4):
        scatter_o.swap(k)
    gather.relay()

    def attended_grad(zz):
        rows = span(256 * zz, 256, 256)
        gatt[rows, :] = dot(g[rows, :], wa[:, 640:896]).astype(bf16)

    gather.have_own()
    attended_grad(z)
    gather.share()
    gather.have_dn()
    attended_grad(dn)
    gather.have_up()
    attended_grad(up)
    gather.share_far()
    planes_b.relay()
    for k in range(3):
        scatter_o.add(k)
    gather.have_far()
    attended_grad(far)

    def pair(i, h, which, k, diagonal):
        rows, cols = pl.ds(256 * i, 256), pl.ds(128 * h, 128)
        source = okv_ref if which else kv_ref
        keys = span(256 * k, 256, 256)
        s = dot_nt(source[keys, 0:128], q_ref[rows, cols])
        ok = segment_of(column(256 * k + (0 if which else here), 256), counts) == segment_of(
            line(256 * i + here, 256), counts
        )
        if diagonal:
            ok &= lax.broadcasted_iota(jnp.int32, (256, 256), 1) >= lax.broadcasted_iota(
                jnp.int32, (256, 256), 0
            )
        w = jnp.where(ok, jnp.exp2(s * (SCALE * LOG2E)), 0.0)
        return w, dot_nt(source[keys, 128:256], gatt[rows, cols])

    def count(w, gw):
        tot[...] += jnp.sum(w, axis=0, keepdims=True)
        inn[...] += jnp.sum(w * gw, axis=0, keepdims=True)

    def weigh_back(i, h, which, k, diagonal):
        at = span(256 * k, 256, 256)
        w, gw = pair(i, h, which, k, diagonal)
        count(w, gw)
        ps[at] = w
        gps[at] = gw

    def spread(i, h, which, k):
        rows, cols = pl.ds(256 * i, 256), pl.ds(128 * h, 128)
        source, out = (okv_ref, gokv) if which else (kv_ref, gkv)
        keys = at = span(256 * k, 256, 256)
        w = ps[at] * tot[...]
        ds = (w * (gps[at] - inn[...]) * SCALE).astype(bf16)
        out[keys, 0:128] += dot(ds, q_ref[rows, cols])
        out[keys, 128:256] += dot(w.astype(bf16), gatt[rows, cols])
        gq[rows, cols] += dot_tn(ds, source[keys, 0:128])

    def settle():
        inv = 1.0 / tot[...]
        tot[...] = inv
        inn[...] = inn[...] * inv

    def clear():
        tot[...] = jnp.zeros_like(tot)
        inn[...] = jnp.zeros_like(inn)

    @pl.when(yh == 1)
    def _():
        for i in range(4):
            for h in range(2):
                clear()
                for k in range(i + 1):
                    count(*pair(i, h, 0, k, k == i))

                def first(k, carry):
                    weigh_back(i, h, 1, k, False)
                    return carry

                def second(k, carry):
                    spread(i, h, 1, k)
                    return carry

                lax.fori_loop(0, 4, first, 0)
                settle()
                tots[2 * i + h] = tot[...]
                inns[2 * i + h] = inn[...]
                lax.fori_loop(0, 4, second, 0)

        def body(r):
            give[r] = gokv[r].astype(bf16)

        by_rows(HALF_KEYS, body, 64)
        give_kv.start()

    for i in range(4):
        for h in range(2):
            clear()
            for k in range(i + 1):
                weigh_back(i, h, 0, k, k == i)
            settle()

            @pl.when(yh == 1)
            def _():
                tot[...] = tots[2 * i + h]
                inn[...] = inns[2 * i + h]

            for k in range(i + 1):
                spread(i, h, 0, k)
        if i == 1:
            scatter_o.relay()
        if i == 2:
            planes_b.turn()

    def back_head(r, h, grad):
        v = proj_ref[r, 128 * h : 128 * h + 128]
        k = h // 2
        scale = lax.rsqrt(jnp.mean(v * v, axis=-1, keepdims=True) + EPS)
        hat = v * scale
        du = grad * tab_ref[0, r] + turn(grad * tab_ref[1, r])
        gsum[k : k + 1] += jnp.sum(du * hat, axis=0, keepdims=True)
        dh = du * gains_ref[k : k + 1]
        dv = scale * (dh - hat * jnp.mean(dh * hat, axis=-1, keepdims=True))
        gp[r, 128 * h : 128 * h + 128] = dv.astype(bf16)

    def back_query(r):
        for h in range(2):
            back_head(r, h, gq[r, 128 * h : 128 * h + 128])

    by_rows(HALF_KEYS, back_query, 64)
    planes_b.relay2()
    for k in range(8):
        v = dot_tn(g[:, 256 * k : 256 * k + 256], att_ref[...]).astype(bf16)
        for j in range(2):
            b = 2 * k + j
            pa[b // 4, b % 4, :, 640:896] = v[ROWS * j : ROWS * j + ROWS]
    gather.drain()
    get_n = pltpu.make_async_copy(n_ref, g, sems.at[2])
    get_n.start()
    def close_out(r, t):
        bo_ref[r] = (mid_ref[r] + t).astype(bf16)

    scatter_o.finish(close_out)
    planes_b.finish()
    swap_b.start()

    @pl.when(yh == 0)
    def _():
        give_kv.wait_recv()

        def body(r):
            gkv[r] += take[r].astype(f32)

        by_rows(HALF_KEYS, body, 64)

    def back_key(r):
        back_head(r, 2, gkv[r, 0:128])
        gp[r, 384:512] = gkv[r, 128:256].astype(bf16)

    by_rows(HALF_KEYS, back_key, 64)
    get_n.wait()
    for k in range(8):
        v = dot_tn(g[:, 256 * k : 256 * k + 256], gp[...]).astype(bf16)
        for j in range(2):
            b = 2 * k + j
            pa[b // 4, b % 4, :, 0:512] = v[ROWS * j : ROWS * j + ROWS]
    sums = jnp.concatenate([gsum[...], jnp.zeros((120, 128), f32)], axis=0).astype(bf16)
    col = lax.broadcasted_iota(jnp.int32, (ROWS, 128), 1)
    row = lax.broadcasted_iota(jnp.int32, (ROWS, 128), 0)
    for k in range(16):
        pick = (row + ROWS * k == 16 * col).astype(bf16)
        pa[k // 4, k % 4, :, 512:640] = dot_nt(pick, sums).astype(bf16)
    planes_a.start()
    for k, zz in enumerate(scatter.order):
        rows = span(256 * zz, 256, 256)
        for m in range(4):
            cols = pl.ds(512 * m, 512)
            p[rows, cols] = dot_nt(gp[rows, :], wa[cols, 0:512]).astype(bf16)
        scatter.swap(k)
        if k:
            scatter.add(k - 1)
    planes_a.relay()
    scatter.relay()
    planes_a.turn()
    planes_a.relay2()

    def close(r, t):
        v = tok_ref[r].astype(f32)
        s = lax.rsqrt(jnp.mean(v * v, axis=-1, keepdims=True) + EPS)
        hat = v * s
        tg_ref[r] = gmid_ref[r] + s * (t - hat * jnp.mean(t * hat, axis=-1, keepdims=True))

    planes_a.finish()
    swap_a.start()
    scatter.finish(close)

    @pl.when(yh == 1)
    def _():
        give_kv.wait_send()

    swap_b.finish()
    swap_b.drain()
    swap_a.finish()
    swap_a.drain()
    planes_b.drain()
    planes_a.drain()


def backward(gbr, wa, att, q, kv, okv, counts, proj, tab, gains, part, n, tokens, gmid, po, mid, cid):
    return pl.pallas_call(
        backward_kernel,
        out_shape=(
            struct((ROWS, D), f32),
            struct((ROWS, D), bf16),
            struct((GROUP, 16, A_WIDTH), bf16),
            struct((GROUP, 16, B_WIDTH), bf16),
        ),
        in_specs=[VM, ANY, VM, VM, VM, VM, SM, VM, VM, VM, ANY, ANY, VM, VM, ANY, VM],
        out_specs=(VM, VM, ANY, ANY),
        scratch_shapes=[
            pltpu.VMEM((HALF_KEYS, D), bf16),
            pltpu.VMEM((D, A_WIDTH), bf16),
            pltpu.VMEM((HALF_KEYS, D), bf16),
            pltpu.VMEM((HALF_KEYS, 256), bf16),
            pltpu.VMEM((HALF_KEYS, 256), f32),
            pltpu.VMEM((HALF_KEYS, 256), f32),
            pltpu.VMEM((1, 256), f32),
            pltpu.VMEM((1, 256), f32),
            pltpu.VMEM((8, 1, 256), f32),
            pltpu.VMEM((8, 1, 256), f32),
            pltpu.VMEM((HALF_KEYS, 256), f32),
            pltpu.VMEM((HALF_KEYS, 256), f32),
            pltpu.VMEM((HALF_KEYS, 256), f32),
            pltpu.VMEM((HALF_KEYS, 256), bf16),
            pltpu.VMEM((HALF_KEYS, 256), bf16),
            pltpu.VMEM((HALF_KEYS, 512), bf16),
            pltpu.VMEM((8, 128), f32),
            pltpu.VMEM((4, 4, ROWS, A_WIDTH), bf16),
            DMA((3,)),
            DMA((2,)),
        ]
        + GATHER_SCRATCH
        + SWAP_SCRATCH * 2
        + scatter_scratch()
        + scatter_scratch()[:1]
        + scatter_scratch()[2:]
        + plane_scatter_scratch(B_WIDTH)
        + plane_scatter_scratch(A_WIDTH),
        compiler_params=params(cid, 63),
        name="backward",
    )(gbr, wa, att, q, kv, okv, counts, proj, tab, gains, part.reshape(4, 4, ROWS, B_WIDTH), n, tokens, gmid, po, mid)


def unchunk(g, parts):
    pieces = []
    at = 0
    for width in parts:
        pieces.append(g[:, :, at : at + width].transpose(1, 0, 2).reshape(16, GROUP * width))
        at += width
    return jnp.concatenate(pieces, axis=1)


def local(
    tokens,
    cotangent,
    seq_rows,
    qkv_weight,
    out_weight,
    attn_gain,
    query_gain,
    key_gain,
    gate_up_weight,
    down_weight,
    mlp_gain,
):
    (
        n_full, wa, wb, c_full, m_full, projected, q, kv, other_kv, attended, gains, tables, middle,
    ) = forward(
        tokens,
        qkv_weight,
        out_weight,
        gate_up_weight,
        down_weight,
        attn_gain[None],
        mlp_gain[None],
        query_gain[None],
        key_gain[None],
        cotangent,
        seq_rows,
        0,
    )
    out_partial, g_middle, g_branch, mlp_part = mlp(m_full, middle, cotangent, c_full, wb, 1)
    tokens_grad, block_out, owned, owned_b = backward(
        g_branch, wa, attended, q, kv, other_kv, seq_rows, projected, tables, gains, mlp_part, n_full, tokens, g_middle,
        out_partial, middle, 2,
    )
    owned = owned.astype(f32)
    owned_b = owned_b.astype(f32)
    qkv_raw = unchunk(owned[:, :, :512], (256, 128, 128))
    gain_grads = jnp.sum(owned[:, 0, 512:514], axis=0)
    out_grad = unchunk(owned[:, :, 640:896], (256,))
    gate_up_raw = unchunk(owned_b[:, :, :1536], (768, 768))
    down_grad = unchunk(owned_b[:, :, 1536:], (768,))
    return (
        block_out,
        tokens_grad,
        qkv_raw * attn_gain.astype(f32)[:, None],
        out_grad,
        jnp.sum(qkv_raw * qkv_weight.astype(f32), axis=1),
        gain_grads[:1],
        gain_grads[1:],
        gate_up_raw * mlp_gain.astype(f32)[:, None],
        down_grad,
        jnp.sum(gate_up_raw * gate_up_weight.astype(f32), axis=1),
    )


def solution(mesh):
    fine = Mesh(mesh.devices.reshape(4, 2, 2, 4, 2), AXES)
    rows2 = P(AXES, None)
    rows1 = P(AXES)
    return jax.shard_map(
        local,
        mesh=fine,
        in_specs=(
            rows2,
            rows2,
            P(("x", "yl"), None),
            rows2,
            rows2,
            rows1,
            rows1,
            rows1,
            rows2,
            rows2,
            rows1,
        ),
        out_specs=(
            rows2,
            rows2,
            rows2,
            rows2,
            rows1,
            rows1,
            rows1,
            rows2,
            rows2,
            rows1,
        ),
        check_vma=False,
    )
```
